256 devices in a mesh: seq: 32 (over y, x, core), chan: 8 (over z).
Axes of the slice: x: 4, y: 4, z: 8, core: 2. Of those that a mesh axis runs over, the one named last changes fastest.
Arguments:
- query_in: bfloat16 [16384, 4096], P('seq', 'chan'), may hold values from -6 to 6
- key_in: bfloat16 [16384, 4096], P('seq', 'chan'), may hold values from -6 to 6
- value_in: bfloat16 [16384, 4096], P('seq', 'chan'), may hold values from -6 to 6
- filter_taps: float32 [16384, 4096], P('seq', 'chan'), may hold values from -0.046875 to 0.046875
- skip_gain: float32 [4096], P('chan'), may hold values from 0.5 to 1.5
- out_weight: bfloat16 [4096, 4096], P('chan'), may hold values from -0.125 to 0.125
Outputs:
- mixed: bfloat16 [16384, 4096], P('seq', 'chan')
The draws below stay inside these ranges and needn't reach their ends.
All inputs are finite; a program needn't handle non-finite values.
Results may differ from the reference program's by a relative error of at most 0.0049.
Values sent between devices are 32-bit elements; how exact they have to be, the bound alone decides.
No kernel may reach another device: no remote copies, remote signals or barrier semaphores. Data moves between devices by JAX's collectives and lax.ppermute only.
A program may use at most 128 MiB of HBM per device.

```python
import jax
import jax.numpy as jnp
from jax import lax

D = 4096
SEQ = 16384


def raised(array, rng, source, target, shards_of, factor):
    owner, partner = [(jnp.arange(array.shape[axis_at]) // (array.shape[axis_at] // shards_of)).reshape([-1 if axis == axis_at else 1 for axis in range(array.ndim)]) for axis_at in (source, target)]
    chosen = jax.random.permutation(rng, shards_of)[partner]
    strong = (owner == chosen) | (owner == (partner + shards_of // 2) % shards_of)
    return jnp.where(strong, factor * array, array)


def block_scale(key, extent, cuts, low, largest):
    loudness = 1.0
    for position, blocks in cuts:
        steps = jax.random.uniform(jax.random.fold_in(jax.random.fold_in(key, 6), position), (blocks,), jnp.float32, low / len(cuts), largest / len(cuts))
        loudness = loudness * jnp.repeat(jnp.exp(steps), extent[position] // blocks).reshape((-1,) + (1,) * (len(extent) - 1 - position))
    return loudness


def scatter_about(rng, extent, scale, limit, shards=(), kind=jnp.bfloat16):
    entries = scale * jax.random.normal(rng, extent, jnp.float32)
    if shards:
        entries = entries * block_scale(rng, extent, shards, -0.22, 0.18)
    return jnp.clip(entries, -limit, limit).astype(kind)


def bell_draw_with(key, shape, deviation, most, pieces, heavy, held_as=jnp.bfloat16):
    entries = deviation * jax.random.normal(key, shape, jnp.float32)
    if pieces:
        entries = entries * block_scale(key, shape, pieces, -0.22, 0.18)
    return jnp.clip(raised(entries, jax.random.fold_in(key, 3), *heavy), -most, most).astype(held_as)


def setup_inputs(seed: int = 0) -> dict:
    splits = jax.random.split(jax.random.key(seed), 7)
    query_in = scatter_about(splits[0], (SEQ, D), 1.0, 6.0, ((0, 32), (1, 8)))
    key_in = scatter_about(splits[1], (SEQ, D), 1.0, 6.0, ((0, 32), (1, 8)))
    value_in = scatter_about(splits[2], (SEQ, D), 1.0, 6.0, ((0, 32), (1, 8)))
    filter_taps = scatter_about(splits[3], (SEQ, D), SEQ ** -0.5, 0.046875, ((0, 32), (1, 8)), jnp.float32)
    skip_gain = jnp.clip(0.5 + 1.0 * jax.random.uniform(splits[4], (D,), jnp.float32) ** block_scale(splits[4], (D,), ((0, 8),), -0.2, 0.2), 0.5, 1.5)
    out_weight = bell_draw_with(splits[5], (D, D), D ** -0.5, 0.125, ((0, 8),), (0, 1, 8, 2.0))
    return {"query_in": query_in, "key_in": key_in, "value_in": value_in, "filter_taps": filter_taps, "skip_gain": skip_gain, "out_weight": out_weight}


def conv_block(pair):
    signal_blk, taps_blk = pair
    length = 2 * SEQ
    spec_sig = jnp.fft.rfft(signal_blk, n=length, axis=0)
    spec_taps = jnp.fft.rfft(taps_blk, n=length, axis=0)
    result = jnp.fft.irfft(spec_sig * spec_taps, n=length, axis=0)[:SEQ]
    return result.astype(signal_blk.dtype)


def reference(query_in, key_in, value_in, filter_taps, skip_gain, out_weight):
    signal = key_in.astype(jnp.float32) * value_in.astype(jnp.float32)
    groups_ref = 8
    signal_grp = signal.reshape(SEQ, groups_ref, D // groups_ref).transpose(1, 0, 2)
    taps_grp = filter_taps.reshape(SEQ, groups_ref, D // groups_ref).transpose(1, 0, 2)
    conv_grp = lax.map(conv_block, (signal_grp, taps_grp))
    conv = conv_grp.transpose(1, 0, 2).reshape(SEQ, D)
    response = conv + skip_gain[None, :] * signal
    gated = (query_in.astype(jnp.float32) * response).astype(jnp.bfloat16)
    return jnp.dot(gated, out_weight, preferred_element_type=jnp.float32).astype(jnp.bfloat16)
```

```python
import jax
import jax.numpy as jnp
import ml_dtypes
import numpy as np
from jax import lax
from jax.experimental import pallas as pl
from jax.experimental.pallas import tpu as pltpu
from jax.sharding import PartitionSpec as P

LANES = 128
F32 = jnp.float32
BF16 = jnp.bfloat16
VMEM_BYTES = 48 * 1024 * 1024


def halves(table):
    head = table.astype(ml_dtypes.bfloat16)
    tail = (table - head.astype(np.float64)).astype(ml_dtypes.bfloat16)
    return head, tail


def transform_tables(n_parts):
    size = LANES
    total = size * size
    place = np.arange(size)
    pieces = size // n_parts
    a_of = pieces * (place % n_parts) + place // n_parts
    k1 = np.arange(size)
    coarse = -2.0 * np.pi * ((a_of[None, :] * (4 * k1[:, None] + 1)) % (4 * size)) / (4 * size)
    first = np.concatenate([np.cos(coarse), np.sin(coarse)], 0)
    b_of = np.arange(size)
    turn = -2.0 * np.pi * ((b_of[None, :] * (4 * k1[:, None] + 1)) % (4 * total)) / (4 * total)
    fine = -2.0 * np.pi * ((b_of[:, None] * k1[None, :]) % size) / size
    cos_f, sin_f = np.cos(fine), np.sin(fine)
    second = np.block([[cos_f, sin_f], [-sin_f, cos_f]])
    second_back = np.block([[cos_f.T, -sin_f.T], [sin_f.T, cos_f.T]])
    first_back = np.concatenate([np.cos(coarse).T, np.sin(coarse).T], 1) / total
    return first, np.cos(turn), np.sin(turn), second, second_back, first_back


def split(value):
    head = value.astype(BF16)
    return head, (value - head.astype(F32)).astype(BF16)


def dot(left, right):
    return jnp.dot(left, right, preferred_element_type=F32)


def dot_table_left(table_ref, value):
    head, tail = split(value)
    return dot(table_ref[0], head) + (dot(table_ref[1], head) + dot(table_ref[0], tail))


def dot_table_right(value, table_ref):
    head, tail = split(value)
    return dot(head, table_ref[0]) + (dot(head, table_ref[1]) + dot(tail, table_ref[0]))


def pack_kernel(key_ref, value_ref, taps_ref, out_ref):
    parts, _, _, width, _ = out_ref.shape
    signal = key_ref[...].astype(F32) * value_ref[...].astype(F32)
    out_ref[:, 0, 0] = signal.T.reshape(parts, width, LANES)
    out_ref[:, 1, 0] = taps_ref[...].T.reshape(parts, width, LANES)


def pack(key_in, value_in, filter_taps, n_parts):
    tok_rows, channels = key_in.shape
    pieces = tok_rows // LANES
    width = channels // n_parts
    block = pl.BlockSpec((LANES, channels), lambda j: (j, 0))
    return pl.pallas_call(
        pack_kernel,
        grid=(pieces,),
        in_specs=[block, block, block],
        out_specs=pl.BlockSpec((n_parts, 2, 1, width, LANES), lambda j: (0, 0, j, 0, 0)),
        out_shape=jax.ShapeDtypeStruct((n_parts, 2, pieces, width, LANES), F32),
        compiler_params=pltpu.CompilerParams(vmem_limit_bytes=VMEM_BYTES),
        name="pack",
    )(key_in, value_in, filter_taps)


def conv_kernel(n_parts, width, x_ref, first_ref, cos_ref, sin_ref, second_ref, back2_ref, back1_ref, out_ref):
    pieces = LANES // n_parts
    rows = pieces * width
    cos_t, sin_t = cos_ref[...], sin_ref[...]

    def column(part, channel):
        return jnp.concatenate(
            [
                x_ref[pl.ds(part * rows + j * width + channel, n_parts, stride=2 * rows), :]
                for j in range(pieces)
            ],
            0,
        )

    def spectra(channel):
        both = jnp.concatenate([column(0, channel), column(1, channel)], 1)
        coarse = dot_table_left(first_ref, both)
        turned = []
        for lane in (0, LANES):
            real = coarse[:LANES, lane : lane + LANES]
            imag = coarse[LANES:, lane : lane + LANES]
            turned.append(
                jnp.concatenate([real * cos_t - imag * sin_t, real * sin_t + imag * cos_t], 1)
            )
        full = dot_table_right(jnp.concatenate(turned, 0), second_ref)
        s_re, s_im = full[:LANES, :LANES], full[:LANES, LANES:]
        h_re, h_im = full[LANES:, :LANES], full[LANES:, LANES:]
        return jnp.concatenate([s_re * h_re - s_im * h_im, s_re * h_im + s_im * h_re], 1)

    @pl.loop(0, width // 2)
    def _(pair):
        product = jnp.concatenate([spectra(2 * pair), spectra(2 * pair + 1)], 0)
        back = dot_table_right(product, back2_ref)
        turned = []
        for row in (0, LANES):
            real = back[row : row + LANES, :LANES]
            imag = back[row : row + LANES, LANES:]
            turned.append(
                jnp.concatenate([real * cos_t + imag * sin_t, imag * cos_t - real * sin_t], 0)
            )
        result = dot_table_left(back1_ref, jnp.concatenate(turned, 1))
        for at in range(2):
            for j in range(pieces):
                out_ref[pl.ds(j * width + 2 * pair + at, n_parts, stride=rows), :] = result[
                    j * n_parts : (j + 1) * n_parts, at * LANES : (at + 1) * LANES
                ]


def convolve(moved, n_parts, width):
    first, turn_cos, turn_sin, second, back2, back1 = transform_tables(n_parts)
    tables = [
        jnp.asarray(np.stack(halves(first))),
        jnp.asarray(turn_cos.astype(np.float32)),
        jnp.asarray(turn_sin.astype(np.float32)),
        jnp.asarray(np.stack(halves(second))),
        jnp.asarray(np.stack(halves(back2))),
        jnp.asarray(np.stack(halves(back1))),
    ]
    pieces = LANES // n_parts
    return pl.pallas_call(
        lambda *refs: conv_kernel(n_parts, width, *refs),
        out_shape=jax.ShapeDtypeStruct((n_parts * pieces * width, LANES), F32),
        compiler_params=pltpu.CompilerParams(vmem_limit_bytes=VMEM_BYTES),
        name="convolve",
    )(moved, *tables)


def project_kernel(conv_ref, query_ref, key_ref, value_ref, gain_ref, weight_ref, out_ref):
    parts, _, width, _ = conv_ref.shape
    conv = conv_ref[:, 0].reshape(parts * width, LANES).T
    signal = key_ref[...].astype(F32) * value_ref[...].astype(F32)
    response = conv + gain_ref[...] * signal
    gated = (query_ref[...].astype(F32) * response).astype(BF16)
    out_cols = out_ref.shape[2]
    for z in range(out_ref.shape[0]):
        out_ref[z] = dot(gated, weight_ref[:, z * out_cols : (z + 1) * out_cols])


def project(conv, query_in, key_in, value_in, skip_gain, out_weight, n_chan):
    n_parts, pieces, width, _ = conv.shape
    tok_rows, channels = query_in.shape
    out_cols = out_weight.shape[1] // n_chan
    block = pl.BlockSpec((LANES, channels), lambda j: (j, 0))
    return pl.pallas_call(
        project_kernel,
        grid=(pieces,),
        in_specs=[
            pl.BlockSpec((n_parts, 1, width, LANES), lambda j: (0, j, 0, 0)),
            block,
            block,
            block,
            pl.BlockSpec((1, channels), lambda j: (0, 0)),
            pl.BlockSpec(out_weight.shape, lambda j: (0, 0)),
        ],
        out_specs=pl.BlockSpec((n_chan, LANES, out_cols), lambda j: (0, j, 0)),
        out_shape=jax.ShapeDtypeStruct((n_chan, tok_rows, out_cols), F32),
        compiler_params=pltpu.CompilerParams(vmem_limit_bytes=VMEM_BYTES),
        name="project",
    )(conv, query_in, key_in, value_in, skip_gain.reshape(1, channels), out_weight)


def on_device(query_in, key_in, value_in, filter_taps, skip_gain, out_weight):
    n_parts = lax.axis_size("seq")
    n_chan = lax.axis_size("chan")
    tok_rows, channels = key_in.shape
    pieces = tok_rows // LANES
    width = channels // n_parts
    packed = pack(key_in, value_in, filter_taps, n_parts)
    moved = lax.all_to_all(packed, "seq", split_axis=0, concat_axis=0, tiled=True)
    conv = convolve(moved.reshape(n_parts * 2 * pieces * width, LANES), n_parts, width)
    conv = conv.reshape(n_parts, pieces, width, LANES)
    conv = lax.all_to_all(conv, "seq", split_axis=0, concat_axis=0, tiled=True)
    partial = project(conv, query_in, key_in, value_in, skip_gain, out_weight, n_chan)
    mixed = lax.psum_scatter(partial, "chan", scatter_dimension=0, tiled=True)
    return mixed.reshape(tok_rows, mixed.shape[2]).astype(BF16)


def solution(mesh):
    in_specs = (
        P("seq", "chan"),
        P("seq", "chan"),
        P("seq", "chan"),
        P("seq", "chan"),
        P("chan"),
        P("chan", None),
    )
    return jax.shard_map(
        on_device, mesh=mesh, in_specs=in_specs, out_specs=P("seq", "chan"), check_vma=False
    )
```

```python
import jax
import jax.numpy as jnp
import ml_dtypes
import numpy as np
from jax import lax
from jax.experimental import pallas as pl
from jax.experimental.pallas import tpu as pltpu
from jax.sharding import PartitionSpec as P

LANES = 128
F32 = jnp.float32
BF16 = jnp.bfloat16
VMEM_BYTES = 48 * 1024 * 1024


def halves(table):
    head = table.astype(ml_dtypes.bfloat16)
    tail = (table - head.astype(np.float64)).astype(ml_dtypes.bfloat16)
    return head, tail


def transform_tables(n_parts):
    size = LANES
    total = size * size
    place = np.arange(size)
    pieces = size // n_parts
    a_of = pieces * (place % n_parts) + place // n_parts
    k1 = np.arange(size)
    coarse = -2.0 * np.pi * ((a_of[None, :] * (4 * k1[:, None] + 1)) % (4 * size)) / (4 * size)
    first = np.concatenate([np.cos(coarse), np.sin(coarse)], 0)
    b_of = np.arange(size)
    turn = -2.0 * np.pi * ((b_of[None, :] * (4 * k1[:, None] + 1)) % (4 * total)) / (4 * total)
    fine = -2.0 * np.pi * ((b_of[:, None] * k1[None, :]) % size) / size
    cos_f, sin_f = np.cos(fine), np.sin(fine)
    second = np.block([[cos_f, sin_f], [-sin_f, cos_f]])
    second_back = np.block([[cos_f.T, -sin_f.T], [sin_f.T, cos_f.T]])
    first_back = np.concatenate([np.cos(coarse).T, np.sin(coarse).T], 1) / total
    return first, np.cos(turn), np.sin(turn), second, second_back, first_back


def split(value):
    head = value.astype(BF16)
    return head, (value - head.astype(F32)).astype(BF16)


def dot(left, right):
    return jnp.dot(left, right, preferred_element_type=F32)


def dot_table_left(table_ref, value):
    head, tail = split(value)
    return dot(table_ref[0], head) + (dot(table_ref[1], head) + dot(table_ref[0], tail))


def dot_table_right(value, table_ref):
    head, tail = split(value)
    return dot(head, table_ref[0]) + (dot(head, table_ref[1]) + dot(tail, table_ref[0]))


def pack_kernel(key_ref, value_ref, taps_ref, out_ref):
    parts, _, _, width, _ = out_ref.shape
    signal = key_ref[...].astype(F32) * value_ref[...].astype(F32)
    out_ref[:, 0, 0] = signal.T.reshape(parts, width, LANES)
    out_ref[:, 1, 0] = taps_ref[...].T.reshape(parts, width, LANES)


def pack(key_in, value_in, filter_taps, n_parts):
    tok_rows, channels = key_in.shape
    pieces = tok_rows // LANES
    width = channels // n_parts
    block = pl.BlockSpec((LANES, channels), lambda j: (j, 0))
    return pl.pallas_call(
        pack_kernel,
        grid=(pieces,),
        in_specs=[block, block, block],
        out_specs=pl.BlockSpec((n_parts, 2, 1, width, LANES), lambda j: (0, 0, j, 0, 0)),
        out_shape=jax.ShapeDtypeStruct((n_parts, 2, pieces, width, LANES), F32),
        compiler_params=pltpu.CompilerParams(vmem_limit_bytes=VMEM_BYTES),
        name="pack",
    )(key_in, value_in, filter_taps)


def conv_kernel(n_parts, width, x_ref, first_ref, cos_ref, sin_ref, second_ref, back2_ref, back1_ref, out_ref):
    pieces = LANES // n_parts
    rows = pieces * width
    cos_t, sin_t = cos_ref[...], sin_ref[...]

    def column(part, channel):
        return jnp.concatenate(
            [
                x_ref[pl.ds(part * rows + j * width + channel, n_parts, stride=2 * rows), :]
                for j in range(pieces)
            ],
            0,
        )

    def spectra(channel):
        both = jnp.concatenate([column(0, channel), column(1, channel)], 1)
        coarse = dot_table_left(first_ref, both)
        turned = []
        for lane in (0, LANES):
            real = coarse[:LANES, lane : lane + LANES]
            imag = coarse[LANES:, lane : lane + LANES]
            turned.append(
                jnp.concatenate([real * cos_t - imag * sin_t, real * sin_t + imag * cos_t], 1)
            )
        full = dot_table_right(jnp.concatenate(turned, 0), second_ref)
        s_re, s_im = full[:LANES, :LANES], full[:LANES, LANES:]
        h_re, h_im = full[LANES:, :LANES], full[LANES:, LANES:]
        return jnp.concatenate([s_re * h_re - s_im * h_im, s_re * h_im + s_im * h_re], 1)

    @pl.loop(0, width // 2)
    def _(pair):
        product = jnp.concatenate([spectra(2 * pair), spectra(2 * pair + 1)], 0)
        back = dot_table_right(product, back2_ref)
        turned = []
        for row in (0, LANES):
            real = back[row : row + LANES, :LANES]
            imag = back[row : row + LANES, LANES:]
            turned.append(
                jnp.concatenate([real * cos_t + imag * sin_t, imag * cos_t - real * sin_t], 0)
            )
        result = dot_table_left(back1_ref, jnp.concatenate(turned, 1))
        for at in range(2):
            for j in range(pieces):
                out_ref[pl.ds(j * width + 2 * pair + at, n_parts, stride=rows), :] = result[
                    j * n_parts : (j + 1) * n_parts, at * LANES : (at + 1) * LANES
                ]


def convolve(moved, n_parts, width):
    first, turn_cos, turn_sin, second, back2, back1 = transform_tables(n_parts)
    tables = [
        jnp.asarray(np.stack(halves(first))),
        jnp.asarray(turn_cos.astype(np.float32)),
        jnp.asarray(turn_sin.astype(np.float32)),
        jnp.asarray(np.stack(halves(second))),
        jnp.asarray(np.stack(halves(back2))),
        jnp.asarray(np.stack(halves(back1))),
    ]
    pieces = LANES // n_parts
    return pl.pallas_call(
        lambda *refs: conv_kernel(n_parts, width, *refs),
        out_shape=jax.ShapeDtypeStruct((n_parts * pieces * width, LANES), F32),
        compiler_params=pltpu.CompilerParams(vmem_limit_bytes=VMEM_BYTES),
        name="convolve",
    )(moved, *tables)


def gate_kernel(conv_ref, query_ref, key_ref, value_ref, gain_ref, out_ref):
    parts, _, width, _ = conv_ref.shape
    conv = conv_ref[:, 0].reshape(parts * width, LANES).T
    signal = key_ref[...].astype(F32) * value_ref[...].astype(F32)
    response = conv + gain_ref[...] * signal
    out_ref[...] = (query_ref[...].astype(F32) * response).astype(BF16)


def gate(conv, first, query_in, key_in, value_in, skip_gain):
    n_parts, pieces, width, _ = conv.shape
    channels = query_in.shape[1]
    block = pl.BlockSpec((LANES, channels), lambda j: (j + first, 0))
    return pl.pallas_call(
        gate_kernel,
        grid=(pieces,),
        in_specs=[
            pl.BlockSpec((n_parts, 1, width, LANES), lambda j: (0, j, 0, 0)),
            block,
            block,
            block,
            pl.BlockSpec((1, channels), lambda j: (0, 0)),
        ],
        out_specs=pl.BlockSpec((LANES, channels), lambda j: (j, 0)),
        out_shape=jax.ShapeDtypeStruct((pieces * LANES, channels), BF16),
        compiler_params=pltpu.CompilerParams(vmem_limit_bytes=VMEM_BYTES),
        name="gate",
    )(conv, query_in, key_in, value_in, skip_gain.reshape(1, channels))


def ring_sum(gated, weights, way):
    n_chan = len(weights)
    hops = [(i, (i + way) % n_chan) for i in range(n_chan)]
    total = dot(gated, weights[0])
    for step in range(1, n_chan):
        got = lax.ppermute(total, "chan", hops)
        total = got + dot(gated, weights[step])
    return total


def on_device(query_in, key_in, value_in, filter_taps, skip_gain, out_weight):
    n_parts = lax.axis_size("seq")
    n_chan = lax.axis_size("chan")
    tok_rows, channels = key_in.shape
    pieces = tok_rows // LANES
    width = channels // n_parts
    packed = pack(key_in, value_in, filter_taps, n_parts)
    moved = lax.all_to_all(packed, "seq", split_axis=0, concat_axis=0, tiled=True)
    conv = convolve(moved.reshape(n_parts * 2 * pieces * width, LANES), n_parts, width)
    conv = conv.reshape(n_parts, pieces, width, LANES)
    me = lax.axis_index("chan")
    out_cols = out_weight.shape[1] // n_chan

    def columns(of):
        start = lax.rem(of + 2 * n_chan, n_chan) * out_cols
        return lax.dynamic_slice(out_weight, (0, start), (channels, out_cols))

    down = [columns(me - 1 - step) for step in range(n_chan)]
    up = [down[n_chan - 2 - step] for step in range(n_chan - 1)] + [down[n_chan - 1]]
    rows = []
    half = pieces // 2
    for first in (0, half):
        part = lax.all_to_all(conv[:, first : first + half], "seq", split_axis=0, concat_axis=0, tiled=True)
        gated = gate(part, first, query_in, key_in, value_in, skip_gain)
        middle = half * LANES // 2
        rows.append(ring_sum(gated[:middle], down, 1))
        rows.append(ring_sum(gated[middle:], up, -1))
    return jnp.concatenate(rows, 0).astype(BF16)


def solution(mesh):
    in_specs = (
        P("seq", "chan"),
        P("seq", "chan"),
        P("seq", "chan"),
        P("seq", "chan"),
        P("chan"),
        P("chan", None),
    )
    return jax.shard_map(
        on_device, mesh=mesh, in_specs=in_specs, out_specs=P("seq", "chan"), check_vma=False
    )
```

```python
import jax
import jax.numpy as jnp
import ml_dtypes
import numpy as np
from jax import lax
from jax.experimental import pallas as pl
from jax.experimental.pallas import tpu as pltpu
from jax.sharding import PartitionSpec as P

LANES = 128
F32 = jnp.float32
BF16 = jnp.bfloat16
VMEM_BYTES = 48 * 1024 * 1024


def halves(table):
    head = table.astype(ml_dtypes.bfloat16)
    tail = (table - head.astype(np.float64)).astype(ml_dtypes.bfloat16)
    return head, tail


def transform_tables(n_parts):
    size = LANES
    total = size * size
    place = np.arange(size)
    pieces = size // n_parts
    a_of = pieces * (place % n_parts) + place // n_parts
    k1 = np.arange(size)
    coarse = -2.0 * np.pi * ((a_of[None, :] * (4 * k1[:, None] + 1)) % (4 * size)) / (4 * size)
    first = np.concatenate([np.cos(coarse), np.sin(coarse)], 0)
    b_of = np.arange(size)
    turn = -2.0 * np.pi * ((b_of[None, :] * (4 * k1[:, None] + 1)) % (4 * total)) / (4 * total)
    fine = -2.0 * np.pi * ((b_of[:, None] * k1[None, :]) % size) / size
    cos_f, sin_f = np.cos(fine), np.sin(fine)
    second = np.block([[cos_f, sin_f], [-sin_f, cos_f]])
    second_back = np.block([[cos_f.T, -sin_f.T], [sin_f.T, cos_f.T]])
    first_back = np.concatenate([np.cos(coarse).T, np.sin(coarse).T], 1) / total
    return first, np.cos(turn), np.sin(turn), second, second_back, first_back


def split(value):
    head = value.astype(BF16)
    return head, (value - head.astype(F32)).astype(BF16)


def dot(left, right):
    return jnp.dot(left, right, preferred_element_type=F32)


def dot_table_left(table_ref, value):
    head, tail = split(value)
    return dot(table_ref[0], head) + (dot(table_ref[1], head) + dot(table_ref[0], tail))


def dot_table_right(value, table_ref):
    head, tail = split(value)
    return dot(head, table_ref[0]) + (dot(head, table_ref[1]) + dot(tail, table_ref[0]))


def pack_kernel(key_ref, value_ref, taps_ref, out_ref):
    parts, _, _, width, _ = out_ref.shape
    signal = key_ref[...].astype(F32) * value_ref[...].astype(F32)
    out_ref[:, 0, 0] = signal.T.reshape(parts, width, LANES)
    out_ref[:, 1, 0] = taps_ref[...].T.reshape(parts, width, LANES)


def pack(key_in, value_in, filter_taps, n_parts):
    tok_rows, channels = key_in.shape
    pieces = tok_rows // LANES
    width = channels // n_parts
    block = pl.BlockSpec((LANES, channels), lambda j: (j, 0))
    key_in, value_in, filter_taps = (
        pltpu.with_memory_space_constraint(x, pltpu.HBM) for x in (key_in, value_in, filter_taps)
    )
    return pl.pallas_call(
        pack_kernel,
        grid=(pieces,),
        in_specs=[block, block, block],
        out_specs=pl.BlockSpec((n_parts, 2, 1, width, LANES), lambda j: (0, 0, j, 0, 0)),
        out_shape=jax.ShapeDtypeStruct((n_parts, 2, pieces, width, LANES), F32),
        compiler_params=pltpu.CompilerParams(vmem_limit_bytes=VMEM_BYTES),
        name="pack",
    )(key_in, value_in, filter_taps)


def conv_kernel(n_parts, width, x_ref, first_ref, cos_ref, sin_ref, second_ref, back2_ref, back1_ref, out_ref):
    pieces = LANES // n_parts
    rows = pieces * width
    cos_t, sin_t = cos_ref[...], sin_ref[...]

    def column(part, channel):
        return jnp.concatenate(
            [
                x_ref[pl.ds(part * rows + j * width + channel, n_parts, stride=2 * rows), :]
                for j in range(pieces)
            ],
            0,
        )

    def spectra(channel):
        both = jnp.concatenate([column(0, channel), column(1, channel)], 1)
        coarse = dot_table_left(first_ref, both)
        turned = []
        for lane in (0, LANES):
            real = coarse[:LANES, lane : lane + LANES]
            imag = coarse[LANES:, lane : lane + LANES]
            turned.append(
                jnp.concatenate([real * cos_t - imag * sin_t, real * sin_t + imag * cos_t], 1)
            )
        full = dot_table_right(jnp.concatenate(turned, 0), second_ref)
        s_re, s_im = full[:LANES, :LANES], full[:LANES, LANES:]
        h_re, h_im = full[LANES:, :LANES], full[LANES:, LANES:]
        return jnp.concatenate([s_re * h_re - s_im * h_im, s_re * h_im + s_im * h_re], 1)

    @pl.loop(0, width // 2)
    def _(pair):
        product = jnp.concatenate([spectra(2 * pair), spectra(2 * pair + 1)], 0)
        back = dot_table_right(product, back2_ref)
        turned = []
        for row in (0, LANES):
            real = back[row : row + LANES, :LANES]
            imag = back[row : row + LANES, LANES:]
            turned.append(
                jnp.concatenate([real * cos_t + imag * sin_t, imag * cos_t - real * sin_t], 0)
            )
        result = dot_table_left(back1_ref, jnp.concatenate(turned, 1))
        for at in range(2):
            for j in range(pieces):
                out_ref[pl.ds(j * width + 2 * pair + at, n_parts, stride=rows), :] = result[
                    j * n_parts : (j + 1) * n_parts, at * LANES : (at + 1) * LANES
                ]


def convolve(moved, n_parts, width):
    first, turn_cos, turn_sin, second, back2, back1 = transform_tables(n_parts)
    tables = [
        jnp.asarray(np.stack(halves(first))),
        jnp.asarray(turn_cos.astype(np.float32)),
        jnp.asarray(turn_sin.astype(np.float32)),
        jnp.asarray(np.stack(halves(second))),
        jnp.asarray(np.stack(halves(back2))),
        jnp.asarray(np.stack(halves(back1))),
    ]
    pieces = LANES // n_parts
    return pl.pallas_call(
        lambda *refs: conv_kernel(n_parts, width, *refs),
        out_shape=jax.ShapeDtypeStruct((n_parts * pieces * width, LANES), F32),
        compiler_params=pltpu.CompilerParams(vmem_limit_bytes=VMEM_BYTES),
        name="convolve",
    )(moved, *tables)


def gate_kernel(conv_ref, query_ref, key_ref, value_ref, gain_ref, out_ref):
    parts, _, width, _ = conv_ref.shape
    conv = conv_ref[:, 0].reshape(parts * width, LANES).T
    signal = key_ref[...].astype(F32) * value_ref[...].astype(F32)
    response = conv + gain_ref[...] * signal
    out_ref[...] = (query_ref[...].astype(F32) * response).astype(BF16)


def gate(conv, query_in, key_in, value_in, skip_gain):
    n_parts, pieces, width, _ = conv.shape
    channels = query_in.shape[1]
    block = pl.BlockSpec((LANES, channels), lambda j: (j, 0))
    return pl.pallas_call(
        gate_kernel,
        grid=(pieces,),
        in_specs=[
            pl.BlockSpec((n_parts, 1, width, LANES), lambda j: (0, j, 0, 0)),
            block,
            block,
            block,
            pl.BlockSpec((1, channels), lambda j: (0, 0)),
        ],
        out_specs=pl.BlockSpec((LANES, channels), lambda j: (j, 0)),
        out_shape=jax.ShapeDtypeStruct((pieces * LANES, channels), BF16),
        compiler_params=pltpu.CompilerParams(vmem_limit_bytes=VMEM_BYTES),
        name="gate",
    )(conv, query_in, key_in, value_in, skip_gain.reshape(1, channels))


def ring_sum(gated, weights, way):
    n_chan = len(weights)
    hops = [(i, (i + way) % n_chan) for i in range(n_chan)]
    total = dot(gated, weights[0])
    for step in range(1, n_chan):
        got = lax.ppermute(total, "chan", hops)
        total = got + dot(gated, weights[step])
    return total


def on_device(query_in, key_in, value_in, filter_taps, skip_gain, out_weight):
    n_parts = lax.axis_size("seq")
    n_chan = lax.axis_size("chan")
    tok_rows, channels = key_in.shape
    pieces = tok_rows // LANES
    width = channels // n_parts
    packed = pack(key_in, value_in, filter_taps, n_parts)
    moved = lax.all_to_all(packed, "seq", split_axis=0, concat_axis=0, tiled=True)
    conv = convolve(moved.reshape(n_parts * 2 * pieces * width, LANES), n_parts, width)
    conv = conv.reshape(n_parts, pieces, width, LANES)
    me = lax.axis_index("chan")
    out_cols = out_weight.shape[1] // n_chan

    def columns(of):
        start = lax.rem(of + 2 * n_chan, n_chan) * out_cols
        return lax.dynamic_slice(out_weight, (0, start), (channels, out_cols))

    down = [columns(me - 1 - step) for step in range(n_chan)]
    up = [down[n_chan - 2 - step] for step in range(n_chan - 1)] + [down[n_chan - 1]]
    conv = lax.all_to_all(conv, "seq", split_axis=0, concat_axis=0, tiled=True)
    gated = gate(conv, query_in, key_in, value_in, skip_gain)
    quarter = tok_rows // 4
    rows = [
        ring_sum(gated[i * quarter : (i + 1) * quarter], (down, up)[i % 2], (1, -1)[i % 2])
        for i in range(4)
    ]
    return jnp.concatenate(rows, 0).astype(BF16)


def solution(mesh):
    in_specs = (
        P("seq", "chan"),
        P("seq", "chan"),
        P("seq", "chan"),
        P("seq", "chan"),
        P("chan"),
        P("chan", None),
    )
    return jax.shard_map(
        on_device, mesh=mesh, in_specs=in_specs, out_specs=P("seq", "chan"), check_vma=False
    )
```

```python
import jax
import jax.numpy as jnp
import ml_dtypes
import numpy as np
from jax import lax
from jax.experimental import pallas as pl
from jax.experimental.pallas import tpu as pltpu
from jax.sharding import PartitionSpec as P

LANES = 128
F32 = jnp.float32
BF16 = jnp.bfloat16
VMEM_BYTES = 48 * 1024 * 1024
GROUP = 8


def halves(table):
    head = table.astype(ml_dtypes.bfloat16)
    tail = (table - head.astype(np.float64)).astype(ml_dtypes.bfloat16)
    return head, tail


def transform_tables(n_parts):
    size = LANES
    total = size * size
    place = np.arange(size)
    pieces = size // n_parts
    a_of = pieces * (place % n_parts) + place // n_parts
    k1 = np.arange(size)
    coarse = -2.0 * np.pi * ((a_of[None, :] * (4 * k1[:, None] + 1)) % (4 * size)) / (4 * size)
    first = np.concatenate([np.cos(coarse), np.sin(coarse)], 0)
    b_of = np.arange(size)
    turn = -2.0 * np.pi * ((b_of[None, :] * (4 * k1[:, None] + 1)) % (4 * total)) / (4 * total)
    fine = -2.0 * np.pi * ((b_of[:, None] * k1[None, :]) % size) / size
    cos_f, sin_f = np.cos(fine), np.sin(fine)
    second = np.block([[cos_f, sin_f], [-sin_f, cos_f]])
    second_back = np.block([[cos_f.T, -sin_f.T], [sin_f.T, cos_f.T]])
    first_back = np.concatenate([np.cos(coarse).T, np.sin(coarse).T], 1) / total
    return first, np.cos(turn), np.sin(turn), second, second_back, first_back


def split(value):
    head = value.astype(BF16)
    return head, (value - head.astype(F32)).astype(BF16)


def dot(left, right):
    return jnp.dot(left, right, preferred_element_type=F32)


def tables_of(n_parts):
    first, turn_cos, turn_sin, second, second_back, first_back = transform_tables(n_parts)

    def left(table):
        high, low = halves(table)
        return jnp.asarray(np.concatenate([high, low, high], 1))

    def right(table):
        high, low = halves(table)
        return jnp.asarray(np.concatenate([high, low, high], 0))

    turns = [jnp.asarray(turn_cos.astype(np.float32)), jnp.asarray(turn_sin.astype(np.float32))]
    return [left(first), *turns, right(second), right(second_back), left(first_back)]


def from_left(table, value):
    high, low = split(value)
    return dot(table, jnp.concatenate([high, high, low], 0))


def from_right(value, table):
    high, low = split(value)
    return dot(jnp.concatenate([high, high, low], 1), table)


def pack_kernel(key_ref, value_ref, taps_ref, out_ref):
    parts, _, _, width, _ = out_ref.shape
    signal = key_ref[...].astype(F32) * value_ref[...].astype(F32)
    out_ref[:, 0, 0] = signal.T.reshape(parts, width, LANES)
    out_ref[:, 1, 0] = taps_ref[...].T.reshape(parts, width, LANES)


def pack(key_in, value_in, filter_taps, n_parts):
    tok_rows, span = key_in.shape
    pieces = tok_rows // LANES
    width = span // n_parts
    block = pl.BlockSpec((LANES, span), lambda j: (j, 0))
    return pl.pallas_call(
        pack_kernel,
        grid=(pieces,),
        in_specs=[block, block, block],
        out_specs=pl.BlockSpec((n_parts, 2, 1, width, LANES), lambda j: (0, 0, j, 0, 0)),
        out_shape=jax.ShapeDtypeStruct((n_parts, 2, pieces, width, LANES), F32),
        compiler_params=pltpu.CompilerParams(vmem_limit_bytes=VMEM_BYTES),
        name="pack",
    )(*(pltpu.with_memory_space_constraint(x, pltpu.HBM) for x in (key_in, value_in, filter_taps)))


def conv_kernel(n_parts, width, group, x_ref, first_ref, cos_ref, sin_ref, second_ref, back2_ref, back1_ref, out_ref):
    pieces = LANES // n_parts
    rows = pieces * width
    cos_t, sin_t = cos_ref[...], sin_ref[...]

    def column(part, channel):
        return jnp.concatenate(
            [
                x_ref[pl.ds(part * rows + j * width + channel, n_parts, stride=2 * rows), :]
                for j in range(pieces)
            ],
            0,
        )

    def spectrum(coarse, lane):
        real = coarse[:LANES, lane : lane + LANES]
        imag = coarse[LANES:, lane : lane + LANES]
        return jnp.concatenate([real * cos_t - imag * sin_t, real * sin_t + imag * cos_t], 1)

    def product(pair):
        s_re, s_im = pair[:LANES, :LANES], pair[:LANES, LANES:]
        h_re, h_im = pair[LANES:, :LANES], pair[LANES:, LANES:]
        return jnp.concatenate([s_re * h_re - s_im * h_im, s_re * h_im + s_im * h_re], 1)

    def unturn(back):
        real, imag = back[:, :LANES], back[:, LANES:]
        return jnp.concatenate([real * cos_t + imag * sin_t, imag * cos_t - real * sin_t], 0)

    @pl.loop(0, width // group)
    def _(turn):
        channels = [turn * group + i for i in range(group)]
        coarse = [
            from_left(first_ref[...], jnp.concatenate([column(0, c), column(1, c)], 1))
            for c in channels
        ]
        turned = [spectrum(c, lane) for c in coarse for lane in (0, LANES)]
        full = from_right(jnp.concatenate(turned, 0), second_ref[...])
        products = [product(full[2 * k * LANES : 2 * (k + 1) * LANES]) for k in range(group)]
        back = from_right(jnp.concatenate(products, 0), back2_ref[...])
        columns = [unturn(back[k * LANES : (k + 1) * LANES]) for k in range(group)]
        result = from_left(back1_ref[...], jnp.concatenate(columns, 1))
        for k, channel in enumerate(channels):
            for j in range(pieces):
                out_ref[pl.ds(j * width + channel, n_parts, stride=rows), :] = result[
                    j * n_parts : (j + 1) * n_parts, k * LANES : (k + 1) * LANES
                ]


def convolve(moved, n_parts, width):
    pieces = LANES // n_parts
    group = GROUP if width % GROUP == 0 else 1
    flops = 2 * 3 * LANES * LANES * LANES * width * 18
    return pl.pallas_call(
        lambda *refs: conv_kernel(n_parts, width, group, *refs),
        out_shape=jax.ShapeDtypeStruct((n_parts * pieces * width, LANES), F32),
        compiler_params=pltpu.CompilerParams(vmem_limit_bytes=VMEM_BYTES),
        cost_estimate=pl.CostEstimate(flops=flops, bytes_accessed=moved.size * 6, transcendentals=0),
        name="convolve",
    )(moved, *tables_of(n_parts))


def gate_kernel(conv_ref, query_ref, key_ref, value_ref, gain_ref, out_ref):
    parts, _, width, _ = conv_ref.shape
    conv = conv_ref[:, 0].reshape(parts * width, LANES).T
    signal = key_ref[...].astype(F32) * value_ref[...].astype(F32)
    response = conv + gain_ref[...] * signal
    out_ref[...] = (query_ref[...].astype(F32) * response).astype(BF16)


def gate(conv, query_in, key_in, value_in, skip_gain):
    n_parts, pieces, width, _ = conv.shape
    channels = query_in.shape[1]
    block = pl.BlockSpec((LANES, channels), lambda j: (j, 0))
    return pl.pallas_call(
        gate_kernel,
        grid=(pieces,),
        in_specs=[
            pl.BlockSpec((n_parts, 1, width, LANES), lambda j: (0, j, 0, 0)),
            block,
            block,
            block,
            pl.BlockSpec((1, channels), lambda j: (0, 0)),
        ],
        out_specs=pl.BlockSpec((LANES, channels), lambda j: (j, 0)),
        out_shape=jax.ShapeDtypeStruct((pieces * LANES, channels), BF16),
        compiler_params=pltpu.CompilerParams(vmem_limit_bytes=VMEM_BYTES),
        name="gate",
    )(conv, query_in, key_in, value_in, skip_gain.reshape(1, channels))


def ring_sum(gated, weights, way):
    n_chan = len(weights)
    hops = [(i, (i + way) % n_chan) for i in range(n_chan)]
    total = dot(gated, weights[0])
    for step in range(1, n_chan):
        got = lax.ppermute(total, "chan", hops)
        got, gated = lax.optimization_barrier((got, gated))
        total = got + dot(gated, weights[step])
    return total


def on_device(query_in, key_in, value_in, filter_taps, skip_gain, out_weight):
    n_parts = lax.axis_size("seq")
    n_chan = lax.axis_size("chan")
    tok_rows, channels = key_in.shape
    pieces = tok_rows // LANES
    width = channels // n_parts
    packed = pack(key_in, value_in, filter_taps, n_parts)
    moved = lax.all_to_all(packed, "seq", split_axis=0, concat_axis=0, tiled=True)
    conv = convolve(moved.reshape(-1, LANES), n_parts, width)
    conv = conv.reshape(n_parts, pieces, width, LANES)
    me = lax.axis_index("chan")
    out_cols = out_weight.shape[1] // n_chan

    def columns(of):
        start = lax.rem(of + 2 * n_chan, n_chan) * out_cols
        return lax.dynamic_slice(out_weight, (0, start), (channels, out_cols))

    down = [columns(me - 1 - step) for step in range(n_chan)]
    up = [down[n_chan - 2 - step] for step in range(n_chan - 1)] + [down[n_chan - 1]]
    conv = lax.all_to_all(conv, "seq", split_axis=0, concat_axis=0, tiled=True)
    gated = gate(conv, query_in, key_in, value_in, skip_gain)
    quarter = tok_rows // 4
    rows = [
        ring_sum(gated[i * quarter : (i + 1) * quarter], (down, up)[i % 2], (1, -1)[i % 2])
        for i in range(4)
    ]
    return jnp.concatenate(rows, 0).astype(BF16)


def solution(mesh):
    in_specs = (
        P("seq", "chan"),
        P("seq", "chan"),
        P("seq", "chan"),
        P("seq", "chan"),
        P("chan"),
        P("chan", None),
    )
    return jax.shard_map(
        on_device, mesh=mesh, in_specs=in_specs, out_specs=P("seq", "chan"), check_vma=False
    )
```

```python
import jax
import jax.numpy as jnp
import ml_dtypes
import numpy as np
from jax import lax
from jax.experimental import pallas as pl
from jax.experimental.pallas import tpu as pltpu
from jax.sharding import PartitionSpec as P

LANES = 128
F32 = jnp.float32
BF16 = jnp.bfloat16
SMALL_VMEM = 16 * 1024 * 1024
VMEM_BYTES = 24 * 1024 * 1024
GROUP = 8
SIDE = 4
CORES = 2


def halves(table):
    head = table.astype(ml_dtypes.bfloat16)
    tail = (table - head.astype(np.float64)).astype(ml_dtypes.bfloat16)
    return head, tail


def exchange_order(n_parts):
    gray = (0, 1, 3, 2)
    order = [(gray[y] * SIDE + gray[x]) * CORES + c for y in range(SIDE) for x in range(SIDE) for c in range(CORES)]
    return order if len(order) == n_parts else list(range(n_parts))


def exchange(value, n_parts):
    groups = [exchange_order(n_parts)]
    return lax.all_to_all(value, "seq", split_axis=0, concat_axis=0, tiled=True, axis_index_groups=groups)


def transform_tables(n_parts):
    size = LANES
    total = size * size
    place = np.arange(size)
    pieces = size // n_parts
    a_of = pieces * np.array(exchange_order(n_parts))[place % n_parts] + place // n_parts
    k1 = np.arange(size)
    coarse = -2.0 * np.pi * ((a_of[None, :] * (4 * k1[:, None] + 1)) % (4 * size)) / (4 * size)
    first = np.concatenate([np.cos(coarse), np.sin(coarse)], 0)
    b_of = np.arange(size)
    turn = -2.0 * np.pi * ((b_of[None, :] * (4 * k1[:, None] + 1)) % (4 * total)) / (4 * total)
    fine = -2.0 * np.pi * ((b_of[:, None] * k1[None, :]) % size) / size
    cos_f, sin_f = np.cos(fine), np.sin(fine)
    second = np.block([[cos_f, sin_f], [-sin_f, cos_f]])
    second_back = np.block([[cos_f.T, -sin_f.T], [sin_f.T, cos_f.T]])
    first_back = np.concatenate([np.cos(coarse).T, np.sin(coarse).T], 1) / total
    return first, np.cos(turn), np.sin(turn), second, second_back, first_back


def split(value):
    head = value.astype(BF16)
    return head, (value - head.astype(F32)).astype(BF16)


def dot(left, right):
    return jnp.dot(left, right, preferred_element_type=F32)


def tables_of(n_parts):
    first, turn_cos, turn_sin, second, second_back, first_back = transform_tables(n_parts)

    def left(table):
        high, low = halves(table)
        return jnp.asarray(np.concatenate([high, low, high], 1))

    def right(table):
        high, low = halves(table)
        return jnp.asarray(np.concatenate([high, low, high], 0))

    turns = [jnp.asarray(turn_cos.astype(np.float32)), jnp.asarray(turn_sin.astype(np.float32))]
    return [left(first), *turns, right(second), right(second_back), left(first_back)]


def from_left(table, value):
    high, low = split(value)
    return dot(table, jnp.concatenate([high, high, low], 0))


def from_right(value, table):
    high, low = split(value)
    return dot(jnp.concatenate([high, high, low], 1), table)


def pack_kernel(key_ref, value_ref, taps_ref, out_ref):
    parts, _, pieces, width, _ = out_ref.shape
    for j in range(pieces):
        at = slice(j * LANES, (j + 1) * LANES)
        signal = key_ref[at].astype(F32) * value_ref[at].astype(F32)
        out_ref[:, 0, j] = signal.T.reshape(parts, width, LANES)
        out_ref[:, 1, j] = taps_ref[at].T.reshape(parts, width, LANES)


def pack(key_in, value_in, filter_taps, n_parts):
    tok_rows, span = key_in.shape
    pieces = tok_rows // LANES
    block = pl.BlockSpec((tok_rows, span), lambda i: (0, 0))
    shape = (n_parts, 2, pieces, span // n_parts, LANES)
    return pl.pallas_call(
        pack_kernel,
        grid=(1,),
        in_specs=[block, block, block],
        out_specs=pl.BlockSpec(shape, lambda i: (0, 0, 0, 0, 0)),
        out_shape=jax.ShapeDtypeStruct(shape, F32),
        compiler_params=pltpu.CompilerParams(vmem_limit_bytes=SMALL_VMEM),
        name="pack",
    )(*(pltpu.with_memory_space_constraint(x, pltpu.HBM) for x in (key_in, value_in, filter_taps)))


def conv_kernel(n_parts, width, group, x_ref, first_ref, cos_ref, sin_ref, second_ref, back2_ref, back1_ref, out_ref):
    pieces = LANES // n_parts
    rows = pieces * width
    cos_t, sin_t = cos_ref[...], sin_ref[...]

    def column(part, channel):
        return jnp.concatenate(
            [
                x_ref[pl.ds(part * rows + j * width + channel, n_parts, stride=2 * rows), :]
                for j in range(pieces)
            ],
            0,
        )

    def spectrum(coarse, lane):
        real = coarse[:LANES, lane : lane + LANES]
        imag = coarse[LANES:, lane : lane + LANES]
        return jnp.concatenate([real * cos_t - imag * sin_t, real * sin_t + imag * cos_t], 1)

    def product(pair):
        s_re, s_im = pair[:LANES, :LANES], pair[:LANES, LANES:]
        h_re, h_im = pair[LANES:, :LANES], pair[LANES:, LANES:]
        return jnp.concatenate([s_re * h_re - s_im * h_im, s_re * h_im + s_im * h_re], 1)

    def unturn(back):
        real, imag = back[:, :LANES], back[:, LANES:]
        return jnp.concatenate([real * cos_t + imag * sin_t, imag * cos_t - real * sin_t], 0)

    @pl.loop(0, width // group)
    def _(turn):
        channels = [turn * group + i for i in range(group)]
        coarse = [
            from_left(first_ref[...], jnp.concatenate([column(0, c), column(1, c)], 1))
            for c in channels
        ]
        turned = [spectrum(c, lane) for c in coarse for lane in (0, LANES)]
        full = from_right(jnp.concatenate(turned, 0), second_ref[...])
        products = [product(full[2 * k * LANES : 2 * (k + 1) * LANES]) for k in range(group)]
        back = from_right(jnp.concatenate(products, 0), back2_ref[...])
        columns = [unturn(back[k * LANES : (k + 1) * LANES]) for k in range(group)]
        result = from_left(back1_ref[...], jnp.concatenate(columns, 1))
        for k, channel in enumerate(channels):
            for j in range(pieces):
                out_ref[pl.ds(j * width + channel, n_parts, stride=rows), :] = result[
                    j * n_parts : (j + 1) * n_parts, k * LANES : (k + 1) * LANES
                ]


def convolve(moved, n_parts, width):
    pieces = LANES // n_parts
    group = GROUP if width % GROUP == 0 else 1
    flops = 2 * 3 * LANES * LANES * LANES * width * 18
    return pl.pallas_call(
        lambda *refs: conv_kernel(n_parts, width, group, *refs),
        out_shape=jax.ShapeDtypeStruct((n_parts * pieces * width, LANES), F32),
        compiler_params=pltpu.CompilerParams(vmem_limit_bytes=VMEM_BYTES),
        cost_estimate=pl.CostEstimate(flops=flops, bytes_accessed=moved.size * 6, transcendentals=0),
        name="convolve",
    )(moved, *tables_of(n_parts))


def gate_kernel(conv_ref, query_ref, key_ref, value_ref, gain_ref, out_ref):
    parts, _, width, _ = conv_ref.shape
    conv = conv_ref[:, 0].reshape(parts * width, LANES).T
    signal = key_ref[...].astype(F32) * value_ref[...].astype(F32)
    response = conv + gain_ref[...] * signal
    out_ref[...] = (query_ref[...].astype(F32) * response).astype(BF16)


def gate(conv, query_in, key_in, value_in, skip_gain):
    n_parts, pieces, width, _ = conv.shape
    channels = query_in.shape[1]
    block = pl.BlockSpec((LANES, channels), lambda j: (j, 0))
    return pl.pallas_call(
        gate_kernel,
        grid=(pieces,),
        in_specs=[
            pl.BlockSpec((n_parts, 1, width, LANES), lambda j: (0, j, 0, 0)),
            block,
            block,
            block,
            pl.BlockSpec((1, channels), lambda j: (0, 0)),
        ],
        out_specs=pl.BlockSpec((LANES, channels), lambda j: (j, 0)),
        out_shape=jax.ShapeDtypeStruct((pieces * LANES, channels), BF16),
        compiler_params=pltpu.CompilerParams(vmem_limit_bytes=SMALL_VMEM),
        name="gate",
    )(conv, query_in, key_in, value_in, skip_gain.reshape(1, channels))


def ring_sum(gated, weights, way, start):
    n_chan = len(weights)
    hops = [(i, (i + way) % n_chan) for i in range(n_chan)]
    total = dot(gated, weights[way * start % n_chan])
    for ahead in range(start - 1, -1, -1):
        got = lax.ppermute(total, "chan", hops)
        if ahead == 0:
            return got
        got, gated = lax.optimization_barrier((got, gated))
        total = got + dot(gated, weights[way * ahead % n_chan])


def on_device(query_in, key_in, value_in, filter_taps, skip_gain, out_weight):
    n_parts = lax.axis_size("seq")
    n_chan = lax.axis_size("chan")
    tok_rows, channels = key_in.shape
    pieces = tok_rows // LANES
    width = channels // n_parts
    packed = pack(key_in, value_in, filter_taps, n_parts)
    moved = exchange(packed, n_parts)
    conv = convolve(moved.reshape(-1, LANES), n_parts, width)
    conv = conv.reshape(n_parts, pieces, width, LANES)
    me = lax.axis_index("chan")
    out_cols = out_weight.shape[1] // n_chan
    weights = [
        lax.dynamic_slice(out_weight, (0, (me + k) % n_chan * out_cols), (channels, out_cols))
        for k in range(n_chan)
    ]
    conv = exchange(conv, n_parts)
    conv, weights = lax.optimization_barrier((conv, weights))
    gated = gate(conv, query_in, key_in, value_in, skip_gain)
    rows = []
    half, far = tok_rows // 2, n_chan // 2
    for block, starts in ((gated[:half], (far, far - 1)), (gated[half:], (far - 1, far))):
        up, down = [ring_sum(block, weights, way, start) for way, start in zip((1, -1), starts)]
        up, down, block = lax.optimization_barrier((up, down, block))
        rows.append(up + down + dot(block, weights[0]))
    return jnp.concatenate(rows, 0).astype(BF16)


def solution(mesh):
    in_specs = (
        P("seq", "chan"),
        P("seq", "chan"),
        P("seq", "chan"),
        P("seq", "chan"),
        P("chan"),
        P("chan", None),
    )
    return jax.shard_map(
        on_device, mesh=mesh, in_specs=in_specs, out_specs=P("seq", "chan"), check_vma=False
    )
```

```python
import jax
import jax.numpy as jnp
import ml_dtypes
import numpy as np
from jax import lax
from jax.experimental import pallas as pl
from jax.experimental.pallas import tpu as pltpu
from jax.sharding import PartitionSpec as P

LANES = 128
F32 = jnp.float32
BF16 = jnp.bfloat16
SMALL_VMEM = 16 * 1024 * 1024
VMEM_BYTES = 24 * 1024 * 1024
GROUP = 16
SIDE = 4
CORES = 2


def halves(table):
    head = table.astype(ml_dtypes.bfloat16)
    tail = (table - head.astype(np.float64)).astype(ml_dtypes.bfloat16)
    return head, tail


def exchange_order(n_parts):
    gray = (0, 1, 3, 2)
    order = [(gray[y] * SIDE + gray[x]) * CORES + c for y in range(SIDE) for x in range(SIDE) for c in range(CORES)]
    return order if len(order) == n_parts else list(range(n_parts))


def exchange(value, n_parts):
    groups = [exchange_order(n_parts)]
    return lax.all_to_all(value, "seq", split_axis=0, concat_axis=0, tiled=True, axis_index_groups=groups)


def transform_tables(n_parts):
    size = LANES
    total = size * size
    place = np.arange(size)
    pieces = size // n_parts
    a_of = pieces * np.array(exchange_order(n_parts))[place % n_parts] + place // n_parts
    k1 = np.arange(size)
    coarse = -2.0 * np.pi * ((a_of[None, :] * (4 * k1[:, None] + 1)) % (4 * size)) / (4 * size)
    first = np.concatenate([np.cos(coarse), np.sin(coarse)], 0)
    b_of = np.arange(size)
    turn = -2.0 * np.pi * ((b_of[None, :] * (4 * k1[:, None] + 1)) % (4 * total)) / (4 * total)
    fine = -2.0 * np.pi * ((b_of[:, None] * k1[None, :]) % size) / size
    cos_f, sin_f = np.cos(fine), np.sin(fine)
    second = np.block([[cos_f, sin_f], [-sin_f, cos_f]])
    second_back = np.block([[cos_f.T, -sin_f.T], [sin_f.T, cos_f.T]])
    first_back = np.concatenate([np.cos(coarse).T, np.sin(coarse).T], 1) / total
    return first, np.cos(turn), np.sin(turn), second, second_back, first_back


def split(value):
    head = value.astype(BF16)
    return head, (value - head.astype(F32)).astype(BF16)


def dot(left, right):
    return jnp.dot(left, right, preferred_element_type=F32)


def tables_of(n_parts):
    first, turn_cos, turn_sin, second, second_back, first_back = transform_tables(n_parts)

    def left(table):
        high, low = halves(table)
        return jnp.asarray(np.concatenate([high, low, high], 1))

    def right(table):
        high, low = halves(table)
        return jnp.asarray(np.concatenate([high, low, high], 0))

    turns = [jnp.asarray(turn_cos.astype(np.float32)), jnp.asarray(turn_sin.astype(np.float32))]
    return [left(first), *turns, right(second), right(second_back), left(first_back)]


def from_left(table, value):
    high, low = split(value)
    return dot(table, jnp.concatenate([high, high, low], 0))


def from_right(value, table):
    high, low = split(value)
    return dot(jnp.concatenate([high, high, low], 1), table)


def pack_kernel(key_ref, value_ref, taps_ref, out_ref, key_vmem, value_vmem, taps_vmem, sems):
    parts, _, pieces, width, _ = out_ref.shape
    pairs = ((key_ref, key_vmem), (value_ref, value_vmem), (taps_ref, taps_vmem))
    rows = [pl.ds(j * LANES, LANES) for j in range(pieces)]
    copies = [
        [pltpu.make_async_copy(x.at[at], y.at[at], sems.at[k, j]) for k, (x, y) in enumerate(pairs)]
        for j, at in enumerate(rows)
    ]
    for piece in copies:
        for copy in piece:
            copy.start()
    for j, at in enumerate(rows):
        for copy in copies[j]:
            copy.wait()
        signal = key_vmem[at].astype(F32) * value_vmem[at].astype(F32)
        out_ref[:, 0, j] = signal.T.reshape(parts, width, LANES)
        out_ref[:, 1, j] = taps_vmem[at].T.reshape(parts, width, LANES)


def pack(key_in, value_in, filter_taps, n_parts):
    tok_rows, span = key_in.shape
    pieces = tok_rows // LANES
    arrays = (key_in, value_in, filter_taps)
    return pl.pallas_call(
        pack_kernel,
        in_specs=[pl.BlockSpec(memory_space=pltpu.HBM)] * 3,
        out_specs=pl.BlockSpec(memory_space=pltpu.VMEM),
        out_shape=jax.ShapeDtypeStruct((n_parts, 2, pieces, span // n_parts, LANES), F32),
        scratch_shapes=[pltpu.VMEM(x.shape, x.dtype) for x in arrays]
        + [pltpu.SemaphoreType.DMA((3, pieces))],
        compiler_params=pltpu.CompilerParams(vmem_limit_bytes=SMALL_VMEM),
        name="pack",
    )(*(pltpu.with_memory_space_constraint(x, pltpu.HBM) for x in arrays))


def conv_kernel(n_parts, width, group, x_ref, first_ref, cos_ref, sin_ref, second_ref, back2_ref, back1_ref, out_ref):
    pieces = LANES // n_parts
    rows = pieces * width
    cos_t, sin_t = cos_ref[...], sin_ref[...]

    def column(part, channel):
        return jnp.concatenate(
            [
                x_ref[pl.ds(part * rows + j * width + channel, n_parts, stride=2 * rows), :]
                for j in range(pieces)
            ],
            0,
        )

    def spectrum(coarse, lane):
        real = coarse[:LANES, lane : lane + LANES]
        imag = coarse[LANES:, lane : lane + LANES]
        return jnp.concatenate([real * cos_t - imag * sin_t, real * sin_t + imag * cos_t], 1)

    def product(pair):
        s_re, s_im = pair[:LANES, :LANES], pair[:LANES, LANES:]
        h_re, h_im = pair[LANES:, :LANES], pair[LANES:, LANES:]
        return jnp.concatenate([s_re * h_re - s_im * h_im, s_re * h_im + s_im * h_re], 1)

    def unturn(back):
        real, imag = back[:, :LANES], back[:, LANES:]
        return jnp.concatenate([real * cos_t + imag * sin_t, imag * cos_t - real * sin_t], 0)

    @pl.loop(0, width // group)
    def _(turn):
        channels = [turn * group + i for i in range(group)]
        coarse = [
            from_left(first_ref[...], jnp.concatenate([column(0, c), column(1, c)], 1))
            for c in channels
        ]
        turned = [spectrum(c, lane) for c in coarse for lane in (0, LANES)]
        full = from_right(jnp.concatenate(turned, 0), second_ref[...])
        products = [product(full[2 * k * LANES : 2 * (k + 1) * LANES]) for k in range(group)]
        back = from_right(jnp.concatenate(products, 0), back2_ref[...])
        columns = [unturn(back[k * LANES : (k + 1) * LANES]) for k in range(group)]
        result = from_left(back1_ref[...], jnp.concatenate(columns, 1))
        for k, channel in enumerate(channels):
            for j in range(pieces):
                out_ref[pl.ds(j * width + channel, n_parts, stride=rows), :] = result[
                    j * n_parts : (j + 1) * n_parts, k * LANES : (k + 1) * LANES
                ]


def convolve(moved, n_parts, width):
    pieces = LANES // n_parts
    group = GROUP if width % GROUP == 0 else 1
    flops = 2 * 3 * LANES * LANES * LANES * width * 18
    return pl.pallas_call(
        lambda *refs: conv_kernel(n_parts, width, group, *refs),
        out_shape=jax.ShapeDtypeStruct((n_parts * pieces * width, LANES), F32),
        compiler_params=pltpu.CompilerParams(vmem_limit_bytes=VMEM_BYTES),
        cost_estimate=pl.CostEstimate(flops=flops, bytes_accessed=moved.size * 6, transcendentals=0),
        name="convolve",
    )(moved, *tables_of(n_parts))


def gate_kernel(conv_ref, query_ref, key_ref, value_ref, gain_ref, out_ref):
    parts, _, width, _ = conv_ref.shape
    conv = conv_ref[:, 0].reshape(parts * width, LANES).T
    signal = key_ref[...].astype(F32) * value_ref[...].astype(F32)
    response = conv + gain_ref[...] * signal
    out_ref[...] = (query_ref[...].astype(F32) * response).astype(BF16)


def gate(conv, query_in, key_in, value_in, skip_gain):
    n_parts, pieces, width, _ = conv.shape
    channels = query_in.shape[1]
    block = pl.BlockSpec((LANES, channels), lambda j: (j, 0))
    return pl.pallas_call(
        gate_kernel,
        grid=(pieces,),
        in_specs=[
            pl.BlockSpec((n_parts, 1, width, LANES), lambda j: (0, j, 0, 0)),
            block,
            block,
            block,
            pl.BlockSpec((1, channels), lambda j: (0, 0)),
        ],
        out_specs=pl.BlockSpec((LANES, channels), lambda j: (j, 0)),
        out_shape=jax.ShapeDtypeStruct((pieces * LANES, channels), BF16),
        compiler_params=pltpu.CompilerParams(vmem_limit_bytes=SMALL_VMEM),
        name="gate",
    )(conv, query_in, key_in, value_in, skip_gain.reshape(1, channels))


def columns_kernel(_, weight_ref, out_ref):
    out_ref[...] = weight_ref[...]


def columns(out_weight, device, out_cols):
    rows = out_weight.shape[0]
    return pl.pallas_call(
        columns_kernel,
        grid_spec=pltpu.PrefetchScalarGridSpec(
            num_scalar_prefetch=1,
            grid=(1,),
            in_specs=[pl.BlockSpec((rows, out_cols), lambda i, at: (0, at[0]))],
            out_specs=pl.BlockSpec((rows, out_cols), lambda i, at: (0, 0)),
        ),
        out_shape=jax.ShapeDtypeStruct((rows, out_cols), out_weight.dtype),
        compiler_params=pltpu.CompilerParams(vmem_limit_bytes=SMALL_VMEM),
        name="columns",
    )(device.astype(jnp.int32).reshape(1), pltpu.with_memory_space_constraint(out_weight, pltpu.HBM))


def ring_sum(gated, weights, way, start):
    n_chan = len(weights)
    hops = [(i, (i + way) % n_chan) for i in range(n_chan)]
    total = dot(gated, weights[way * start % n_chan])
    for ahead in range(start - 1, -1, -1):
        got = lax.ppermute(total, "chan", hops)
        if ahead == 0:
            return got
        got, gated = lax.optimization_barrier((got, gated))
        total = got + dot(gated, weights[way * ahead % n_chan])


def on_device(query_in, key_in, value_in, filter_taps, skip_gain, out_weight):
    n_parts = lax.axis_size("seq")
    n_chan = lax.axis_size("chan")
    tok_rows, channels = key_in.shape
    pieces = tok_rows // LANES
    width = channels // n_parts
    packed = pack(key_in, value_in, filter_taps, n_parts)
    moved = exchange(packed, n_parts)
    conv = convolve(moved.reshape(-1, LANES), n_parts, width)
    conv = conv.reshape(n_parts, pieces, width, LANES)
    me = lax.axis_index("chan")
    out_cols = out_weight.shape[1] // n_chan
    weights = [
        lax.dynamic_slice(out_weight, (0, (me + k) % n_chan * out_cols), (channels, out_cols))
        for k in range(n_chan)
    ]
    weights[n_chan // 2] = columns(out_weight, (me + n_chan // 2) % n_chan, out_cols)
    conv = exchange(conv, n_parts)
    conv, weights = lax.optimization_barrier((conv, weights))
    gated = gate(conv, query_in, key_in, value_in, skip_gain)
    rows = []
    half, far = tok_rows // 2, n_chan // 2
    for block, starts in ((gated[:half], (far, far - 1)), (gated[half:], (far - 1, far))):
        up, down = [ring_sum(block, weights, way, start) for way, start in zip((1, -1), starts)]
        up, down, block = lax.optimization_barrier((up, down, block))
        rows.append(up + down + dot(block, weights[0]))
    return jnp.concatenate(rows, 0).astype(BF16)


def solution(mesh):
    in_specs = (
        P("seq", "chan"),
        P("seq", "chan"),
        P("seq", "chan"),
        P("seq", "chan"),
        P("chan"),
        P("chan", None),
    )
    return jax.shard_map(
        on_device, mesh=mesh, in_specs=in_specs, out_specs=P("seq", "chan"), check_vma=False
    )
```

```python
import jax
import jax.numpy as jnp
import ml_dtypes
import numpy as np
from jax import lax
from jax.experimental import pallas as pl
from jax.experimental.pallas import tpu as pltpu
from jax.sharding import PartitionSpec as P

LANES = 128
F32 = jnp.float32
BF16 = jnp.bfloat16
SMALL_VMEM = 16 * 1024 * 1024
VMEM_BYTES = 24 * 1024 * 1024
GROUP = 16
SIDE = 4
CORES = 2


def halves(table):
    head = table.astype(ml_dtypes.bfloat16)
    tail = (table - head.astype(np.float64)).astype(ml_dtypes.bfloat16)
    return head, tail


def exchange_order(n_parts):
    gray = (0, 1, 3, 2)
    order = [(gray[y] * SIDE + gray[x]) * CORES + c for y in range(SIDE) for x in range(SIDE) for c in range(CORES)]
    return order if len(order) == n_parts else list(range(n_parts))


def exchange(value, n_parts):
    groups = [exchange_order(n_parts)]
    return lax.all_to_all(value, "seq", split_axis=0, concat_axis=0, tiled=True, axis_index_groups=groups)


def transform_tables(n_parts):
    size = LANES
    total = size * size
    place = np.arange(size)
    pieces = size // n_parts
    a_of = pieces * np.array(exchange_order(n_parts))[place % n_parts] + place // n_parts
    k1 = np.arange(size)
    coarse = -2.0 * np.pi * ((a_of[None, :] * (4 * k1[:, None] + 1)) % (4 * size)) / (4 * size)
    first = np.concatenate([np.cos(coarse), np.sin(coarse)], 0)
    b_of = np.arange(size)
    turn = -2.0 * np.pi * ((b_of[None, :] * (4 * k1[:, None] + 1)) % (4 * total)) / (4 * total)
    fine = -2.0 * np.pi * ((b_of[:, None] * k1[None, :]) % size) / size
    cos_f, sin_f = np.cos(fine), np.sin(fine)
    second = np.block([[cos_f, sin_f], [-sin_f, cos_f]])
    second_back = np.block([[cos_f.T, -sin_f.T], [sin_f.T, cos_f.T]])
    first_back = np.concatenate([np.cos(coarse).T, np.sin(coarse).T], 1) / total
    return first, np.cos(turn), np.sin(turn), second, second_back, first_back


def split(value):
    head = value.astype(BF16)
    return head, (value - head.astype(F32)).astype(BF16)


def dot(left, right):
    return jnp.dot(left, right, preferred_element_type=F32)


def tables_of(n_parts):
    first, turn_cos, turn_sin, second, second_back, first_back = transform_tables(n_parts)

    def left(table):
        high, low = halves(table)
        return jnp.asarray(np.concatenate([high, low, high], 1))

    def right(table):
        high, low = halves(table)
        return jnp.asarray(np.concatenate([high, low, high], 0))

    turns = [jnp.asarray(turn_cos.astype(np.float32)), jnp.asarray(turn_sin.astype(np.float32))]
    return [left(first), *turns, right(second), right(second_back), left(first_back)]


def from_left(table, value):
    high, low = split(value)
    return dot(table, jnp.concatenate([high, high, low], 0))


def from_right(value, table):
    high, low = split(value)
    return dot(jnp.concatenate([high, high, low], 1), table)


def pack_kernel(key_ref, value_ref, taps_ref, out_ref, key_vmem, value_vmem, taps_vmem, sems):
    parts, _, pieces, width, _ = out_ref.shape
    pairs = ((key_ref, key_vmem), (value_ref, value_vmem), (taps_ref, taps_vmem))
    rows = [pl.ds(j * LANES, LANES) for j in range(pieces)]
    copies = [
        [pltpu.make_async_copy(x.at[at], y.at[at], sems.at[k, j]) for k, (x, y) in enumerate(pairs)]
        for j, at in enumerate(rows)
    ]
    for piece in copies:
        for copy in piece:
            copy.start()
    for j, at in enumerate(rows):
        for copy in copies[j]:
            copy.wait()
        signal = key_vmem[at].astype(F32) * value_vmem[at].astype(F32)
        out_ref[:, 0, j] = signal.T.reshape(parts, width, LANES)
        out_ref[:, 1, j] = taps_vmem[at].T.reshape(parts, width, LANES)


def pack(key_in, value_in, filter_taps, n_parts):
    tok_rows, span = key_in.shape
    pieces = tok_rows // LANES
    arrays = (key_in, value_in, filter_taps)
    return pl.pallas_call(
        pack_kernel,
        in_specs=[pl.BlockSpec(memory_space=pltpu.HBM)] * 3,
        out_specs=pl.BlockSpec(memory_space=pltpu.VMEM),
        out_shape=jax.ShapeDtypeStruct((n_parts, 2, pieces, span // n_parts, LANES), F32),
        scratch_shapes=[pltpu.VMEM(x.shape, x.dtype) for x in arrays]
        + [pltpu.SemaphoreType.DMA((3, pieces))],
        compiler_params=pltpu.CompilerParams(vmem_limit_bytes=SMALL_VMEM),
        name="pack",
    )(*(pltpu.with_memory_space_constraint(x, pltpu.HBM) for x in arrays))


def conv_kernel(n_parts, width, group, x_ref, first_ref, cos_ref, sin_ref, second_ref, back2_ref, back1_ref, out_ref):
    pieces = LANES // n_parts
    rows = pieces * width
    cos_t, sin_t = cos_ref[...], sin_ref[...]

    def column(part, channel):
        return jnp.concatenate(
            [
                x_ref[pl.ds(part * rows + j * width + channel, n_parts, stride=2 * rows), :]
                for j in range(pieces)
            ],
            0,
        )

    def spectrum(coarse, lane):
        real = coarse[:LANES, lane : lane + LANES]
        imag = coarse[LANES:, lane : lane + LANES]
        return jnp.concatenate([real * cos_t - imag * sin_t, real * sin_t + imag * cos_t], 1)

    def product(pair):
        s_re, s_im = pair[:LANES, :LANES], pair[:LANES, LANES:]
        h_re, h_im = pair[LANES:, :LANES], pair[LANES:, LANES:]
        return jnp.concatenate([s_re * h_re - s_im * h_im, s_re * h_im + s_im * h_re], 1)

    def unturn(back):
        real, imag = back[:, :LANES], back[:, LANES:]
        return jnp.concatenate([real * cos_t + imag * sin_t, imag * cos_t - real * sin_t], 0)

    @pl.loop(0, width // group)
    def _(turn):
        channels = [turn * group + i for i in range(group)]
        coarse = [
            from_left(first_ref[...], jnp.concatenate([column(0, c), column(1, c)], 1))
            for c in channels
        ]
        turned = [jnp.concatenate([spectrum(c, lane) for lane in (0, LANES)], 0) for c in coarse]
        full = [from_right(t, second_ref[...]) for t in turned]
        back = [from_right(product(f), back2_ref[...]) for f in full]
        result = from_left(back1_ref[...], jnp.concatenate([unturn(b) for b in back], 1))
        for k, channel in enumerate(channels):
            for j in range(pieces):
                out_ref[pl.ds(j * width + channel, n_parts, stride=rows), :] = result[
                    j * n_parts : (j + 1) * n_parts, k * LANES : (k + 1) * LANES
                ]


def convolve(moved, n_parts, width):
    pieces = LANES // n_parts
    group = GROUP if width % GROUP == 0 else 1
    flops = 2 * 3 * LANES * LANES * LANES * width * 18
    return pl.pallas_call(
        lambda *refs: conv_kernel(n_parts, width, group, *refs),
        out_shape=jax.ShapeDtypeStruct((n_parts * pieces * width, LANES), F32),
        compiler_params=pltpu.CompilerParams(vmem_limit_bytes=VMEM_BYTES),
        cost_estimate=pl.CostEstimate(flops=flops, bytes_accessed=moved.size * 6, transcendentals=0),
        name="convolve",
    )(moved, *tables_of(n_parts))


def gate_kernel(conv_ref, query_ref, key_ref, value_ref, gain_ref, out_ref):
    parts, pieces, width, _ = conv_ref.shape
    for j in range(pieces):
        at = slice(j * LANES, (j + 1) * LANES)
        conv = conv_ref[:, j].reshape(parts * width, LANES).T
        signal = key_ref[at].astype(F32) * value_ref[at].astype(F32)
        response = conv + gain_ref[...] * signal
        out_ref[at] = (query_ref[at].astype(F32) * response).astype(BF16)


def gate(conv, query_in, key_in, value_in, skip_gain):
    whole = pl.BlockSpec(memory_space=pltpu.VMEM)
    return pl.pallas_call(
        gate_kernel,
        in_specs=[whole] * 5,
        out_specs=whole,
        out_shape=jax.ShapeDtypeStruct(query_in.shape, BF16),
        compiler_params=pltpu.CompilerParams(vmem_limit_bytes=SMALL_VMEM),
        name="gate",
    )(conv, query_in, key_in, value_in, skip_gain.reshape(1, query_in.shape[1]))


def columns_kernel(_, weight_ref, out_ref):
    out_ref[...] = weight_ref[...]


def columns(out_weight, device, out_cols):
    rows = out_weight.shape[0]
    return pl.pallas_call(
        columns_kernel,
        grid_spec=pltpu.PrefetchScalarGridSpec(
            num_scalar_prefetch=1,
            grid=(1,),
            in_specs=[pl.BlockSpec((rows, out_cols), lambda i, at: (0, at[0]))],
            out_specs=pl.BlockSpec((rows, out_cols), lambda i, at: (0, 0)),
        ),
        out_shape=jax.ShapeDtypeStruct((rows, out_cols), out_weight.dtype),
        compiler_params=pltpu.CompilerParams(vmem_limit_bytes=SMALL_VMEM),
        name="columns",
    )(device.astype(jnp.int32).reshape(1), pltpu.with_memory_space_constraint(out_weight, pltpu.HBM))


def ring_sum(gated, weights, way, start):
    n_chan = len(weights)
    hops = [(i, (i + way) % n_chan) for i in range(n_chan)]
    total = dot(gated, weights[way * start % n_chan])
    for ahead in range(start - 1, -1, -1):
        got = lax.ppermute(total, "chan", hops)
        if ahead == 0:
            return got
        got, gated = lax.optimization_barrier((got, gated))
        total = got + dot(gated, weights[way * ahead % n_chan])


def on_device(query_in, key_in, value_in, filter_taps, skip_gain, out_weight):
    n_parts = lax.axis_size("seq")
    n_chan = lax.axis_size("chan")
    tok_rows, channels = key_in.shape
    pieces = tok_rows // LANES
    width = channels // n_parts
    packed = pack(key_in, value_in, filter_taps, n_parts)
    moved = exchange(packed, n_parts)
    conv = convolve(moved.reshape(-1, LANES), n_parts, width)
    conv = conv.reshape(n_parts, pieces, width, LANES)
    me = lax.axis_index("chan")
    out_cols = out_weight.shape[1] // n_chan
    weights = [
        lax.dynamic_slice(out_weight, (0, (me + k) % n_chan * out_cols), (channels, out_cols))
        for k in range(n_chan)
    ]
    weights[n_chan // 2] = columns(out_weight, (me + n_chan // 2) % n_chan, out_cols)
    conv = exchange(conv, n_parts)
    conv, weights = lax.optimization_barrier((conv, weights))
    gated = gate(conv, query_in, key_in, value_in, skip_gain)
    rows = []
    half, far = tok_rows // 2, n_chan // 2
    for block, starts in ((gated[:half], (far, far - 1)), (gated[half:], (far - 1, far))):
        up, down = [ring_sum(block, weights, way, start) for way, start in zip((1, -1), starts)]
        up, down, block = lax.optimization_barrier((up, down, block))
        rows.append(up + down + dot(block, weights[0]))
    return jnp.concatenate(rows, 0).astype(BF16)


def solution(mesh):
    in_specs = (
        P("seq", "chan"),
        P("seq", "chan"),
        P("seq", "chan"),
        P("seq", "chan"),
        P("chan"),
        P("chan", None),
    )
    return jax.shard_map(
        on_device, mesh=mesh, in_specs=in_specs, out_specs=P("seq", "chan"), check_vma=False
    )
```

```python
import jax
import jax.numpy as jnp
import ml_dtypes
import numpy as np
from jax import lax
from jax.experimental import pallas as pl
from jax.experimental.pallas import tpu as pltpu
from jax.sharding import PartitionSpec as P

LANES = 128
F32 = jnp.float32
BF16 = jnp.bfloat16
SMALL_VMEM = 16 * 1024 * 1024
VMEM_BYTES = 24 * 1024 * 1024
GROUP = 16
SIDE = 4
CORES = 2


def halves(table):
    head = table.astype(ml_dtypes.bfloat16)
    tail = (table - head.astype(np.float64)).astype(ml_dtypes.bfloat16)
    return head, tail


def exchange_order(n_parts):
    gray = (0, 1, 3, 2)
    order = [(gray[y] * SIDE + gray[x]) * CORES + c for y in range(SIDE) for x in range(SIDE) for c in range(CORES)]
    return order if len(order) == n_parts else list(range(n_parts))


def exchange(value, n_parts):
    groups = [exchange_order(n_parts)]
    return lax.all_to_all(value, "seq", split_axis=0, concat_axis=0, tiled=True, axis_index_groups=groups)


def transform_tables(n_parts):
    size = LANES
    total = size * size
    place = np.arange(size)
    pieces = size // n_parts
    a_of = pieces * np.array(exchange_order(n_parts))[place % n_parts] + place // n_parts
    k1 = np.arange(size)
    coarse = -2.0 * np.pi * ((a_of[None, :] * (4 * k1[:, None] + 1)) % (4 * size)) / (4 * size)
    first = np.concatenate([np.cos(coarse), np.sin(coarse)], 0)
    b_of = np.arange(size)
    turn = -2.0 * np.pi * ((b_of[None, :] * (4 * k1[:, None] + 1)) % (4 * total)) / (4 * total)
    fine = -2.0 * np.pi * ((b_of[:, None] * k1[None, :]) % size) / size
    cos_f, sin_f = np.cos(fine), np.sin(fine)
    second = np.block([[cos_f, sin_f], [-sin_f, cos_f]])
    second_back = np.block([[cos_f.T, -sin_f.T], [sin_f.T, cos_f.T]])
    first_back = np.concatenate([np.cos(coarse).T, np.sin(coarse).T], 1) / total
    return first, np.cos(turn), np.sin(turn), second, second_back, first_back


def split(value):
    head = value.astype(BF16)
    return head, (value - head.astype(F32)).astype(BF16)


def dot(left, right):
    return jnp.dot(left, right, preferred_element_type=F32)


def tables_of(n_parts):
    first, turn_cos, turn_sin, second, second_back, first_back = transform_tables(n_parts)

    def left(table):
        high, low = halves(table)
        return jnp.asarray(np.concatenate([high, low, high], 1))

    def right(table):
        high, low = halves(table)
        return jnp.asarray(np.concatenate([high, low, high], 0))

    turns = [jnp.asarray(turn_cos.astype(np.float32)), jnp.asarray(turn_sin.astype(np.float32))]
    return [left(first), *turns, right(second), right(second_back), left(first_back)]


def from_left(table, value):
    high, low = split(value)
    return dot(table, jnp.concatenate([high, high, low], 0))


def from_right(value, table):
    high, low = split(value)
    return dot(jnp.concatenate([high, high, low], 1), table)


def pack_kernel(key_ref, value_ref, taps_ref, out_ref, key_vmem, value_vmem, taps_vmem, sems):
    parts, _, pieces, width, _ = out_ref.shape
    pairs = ((key_ref, key_vmem), (value_ref, value_vmem), (taps_ref, taps_vmem))
    rows = [pl.ds(j * LANES, LANES) for j in range(pieces)]
    copies = [
        [pltpu.make_async_copy(x.at[at], y.at[at], sems.at[k, j]) for k, (x, y) in enumerate(pairs)]
        for j, at in enumerate(rows)
    ]
    for piece in copies:
        for copy in piece:
            copy.start()
    for j, at in enumerate(rows):
        for copy in copies[j]:
            copy.wait()
        signal = key_vmem[at].astype(F32) * value_vmem[at].astype(F32)
        out_ref[:, 0, j] = signal.T.reshape(parts, width, LANES)
        out_ref[:, 1, j] = taps_vmem[at].T.reshape(parts, width, LANES)


def pack(key_in, value_in, filter_taps, n_parts):
    tok_rows, span = key_in.shape
    pieces = tok_rows // LANES
    arrays = (key_in, value_in, filter_taps)
    return pl.pallas_call(
        pack_kernel,
        in_specs=[pl.BlockSpec(memory_space=pltpu.HBM)] * 3,
        out_specs=pl.BlockSpec(memory_space=pltpu.VMEM),
        out_shape=jax.ShapeDtypeStruct((n_parts, 2, pieces, span // n_parts, LANES), F32),
        scratch_shapes=[pltpu.VMEM(x.shape, x.dtype) for x in arrays]
        + [pltpu.SemaphoreType.DMA((3, pieces))],
        compiler_params=pltpu.CompilerParams(vmem_limit_bytes=SMALL_VMEM),
        name="pack",
    )(*(pltpu.with_memory_space_constraint(x, pltpu.HBM) for x in arrays))


def conv_kernel(n_parts, width, group, x_ref, first_ref, cos_ref, sin_ref, second_ref, back2_ref, back1_ref, out_ref):
    pieces = LANES // n_parts
    rows = pieces * width
    cos_t, sin_t = cos_ref[...], sin_ref[...]

    def column(part, channel):
        return jnp.concatenate(
            [
                x_ref[pl.ds(part * rows + j * width + channel, n_parts, stride=2 * rows), :]
                for j in range(pieces)
            ],
            0,
        )

    def spectrum(coarse, lane):
        real = coarse[:LANES, lane : lane + LANES]
        imag = coarse[LANES:, lane : lane + LANES]
        return jnp.concatenate([real * cos_t - imag * sin_t, real * sin_t + imag * cos_t], 1)

    def product(pair):
        s_re, s_im = pair[:LANES, :LANES], pair[:LANES, LANES:]
        h_re, h_im = pair[LANES:, :LANES], pair[LANES:, LANES:]
        return jnp.concatenate([s_re * h_re - s_im * h_im, s_re * h_im + s_im * h_re], 1)

    def unturn(back):
        real, imag = back[:, :LANES], back[:, LANES:]
        return jnp.concatenate([real * cos_t + imag * sin_t, imag * cos_t - real * sin_t], 0)

    @pl.loop(0, width // group)
    def _(turn):
        channels = [turn * group + i for i in range(group)]
        coarse = [
            from_left(first_ref[...], jnp.concatenate([column(0, c), column(1, c)], 1))
            for c in channels
        ]
        turned = [jnp.concatenate([spectrum(c, lane) for lane in (0, LANES)], 0) for c in coarse]
        full = [from_right(t, second_ref[...]) for t in turned]
        back = [from_right(product(f), back2_ref[...]) for f in full]
        result = from_left(back1_ref[...], jnp.concatenate([unturn(b) for b in back], 1))
        for k, channel in enumerate(channels):
            for j in range(pieces):
                out_ref[pl.ds(j * width + channel, n_parts, stride=rows), :] = result[
                    j * n_parts : (j + 1) * n_parts, k * LANES : (k + 1) * LANES
                ]


def convolve(moved, n_parts, width):
    pieces = LANES // n_parts
    group = GROUP if width % GROUP == 0 else 1
    flops = 2 * 3 * LANES * LANES * LANES * width * 18
    return pl.pallas_call(
        lambda *refs: conv_kernel(n_parts, width, group, *refs),
        out_shape=jax.ShapeDtypeStruct((n_parts * pieces * width, LANES), F32),
        compiler_params=pltpu.CompilerParams(vmem_limit_bytes=VMEM_BYTES),
        cost_estimate=pl.CostEstimate(flops=flops, bytes_accessed=moved.size * 6, transcendentals=0),
        name="convolve",
    )(moved, *tables_of(n_parts))


def gate_kernel(conv_ref, query_ref, key_ref, value_ref, gain_ref, out_ref):
    parts, pieces, width, _ = conv_ref.shape
    for j in range(pieces):
        at = slice(j * LANES, (j + 1) * LANES)
        conv = conv_ref[:, j].reshape(parts * width, LANES).T
        signal = key_ref[at].astype(F32) * value_ref[at].astype(F32)
        response = conv + gain_ref[...] * signal
        out_ref[at] = (query_ref[at].astype(F32) * response).astype(BF16)


def gate(conv, query_in, key_in, value_in, skip_gain):
    whole = pl.BlockSpec(memory_space=pltpu.VMEM)
    return pl.pallas_call(
        gate_kernel,
        in_specs=[whole] * 5,
        out_specs=whole,
        out_shape=jax.ShapeDtypeStruct(query_in.shape, BF16),
        compiler_params=pltpu.CompilerParams(vmem_limit_bytes=SMALL_VMEM),
        name="gate",
    )(conv, query_in, key_in, value_in, skip_gain.reshape(1, query_in.shape[1]))


def columns_kernel(_, weight_ref, out_ref):
    out_ref[...] = weight_ref[...]


def columns(out_weight, device, out_cols):
    rows = out_weight.shape[0]
    return pl.pallas_call(
        columns_kernel,
        grid_spec=pltpu.PrefetchScalarGridSpec(
            num_scalar_prefetch=1,
            grid=(1,),
            in_specs=[pl.BlockSpec((rows, out_cols), lambda i, at: (0, at[0]))],
            out_specs=pl.BlockSpec((rows, out_cols), lambda i, at: (0, 0)),
        ),
        out_shape=jax.ShapeDtypeStruct((rows, out_cols), out_weight.dtype),
        compiler_params=pltpu.CompilerParams(vmem_limit_bytes=SMALL_VMEM),
        name="columns",
    )(device.astype(jnp.int32).reshape(1), pltpu.with_memory_space_constraint(out_weight, pltpu.HBM))


def ring_sum(gated, weights, way, start):
    n_chan = len(weights)
    hops = [(i, (i + way) % n_chan) for i in range(n_chan)]
    total = dot(gated, weights[way * start % n_chan])
    for ahead in range(start - 1, -1, -1):
        got = lax.ppermute(total, "chan", hops)
        if ahead == 0:
            return got
        got, gated = lax.optimization_barrier((got, gated))
        total = got + dot(gated, weights[way * ahead % n_chan])


def join_kernel(upper_ref, lower_ref, out_ref):
    half = upper_ref.shape[0]
    out_ref[:half] = upper_ref[...]
    out_ref[half:] = lower_ref[...]


def join(upper, lower):
    whole = pl.BlockSpec(memory_space=pltpu.VMEM)
    return pl.pallas_call(
        join_kernel,
        in_specs=[whole] * 2,
        out_specs=whole,
        out_shape=jax.ShapeDtypeStruct((2 * upper.shape[0], upper.shape[1]), upper.dtype),
        compiler_params=pltpu.CompilerParams(vmem_limit_bytes=SMALL_VMEM),
        name="join",
    )(upper, lower)


def on_device(query_in, key_in, value_in, filter_taps, skip_gain, out_weight):
    n_parts = lax.axis_size("seq")
    n_chan = lax.axis_size("chan")
    tok_rows, channels = key_in.shape
    pieces = tok_rows // LANES
    width = channels // n_parts
    packed = pack(key_in, value_in, filter_taps, n_parts)
    moved = exchange(packed, n_parts)
    conv = convolve(moved.reshape(-1, LANES), n_parts, width)
    conv = conv.reshape(n_parts, pieces, width, LANES)
    me = lax.axis_index("chan")
    out_cols = out_weight.shape[1] // n_chan
    weights = [
        lax.dynamic_slice(out_weight, (0, (me + k) % n_chan * out_cols), (channels, out_cols))
        for k in range(n_chan)
    ]
    weights[n_chan // 2] = columns(out_weight, (me + n_chan // 2) % n_chan, out_cols)
    conv = exchange(conv, n_parts)
    conv, weights = lax.optimization_barrier((conv, weights))
    gated = gate(conv, query_in, key_in, value_in, skip_gain)
    rows = []
    half, far = tok_rows // 2, n_chan // 2
    for block, starts in ((gated[:half], (far, far - 1)), (gated[half:], (far - 1, far))):
        up, down = [ring_sum(block, weights, way, start) for way, start in zip((1, -1), starts)]
        up, down, block = lax.optimization_barrier((up, down, block))
        rows.append((up + down + dot(block, weights[0])).astype(BF16))
    return join(*rows)


def solution(mesh):
    in_specs = (
        P("seq", "chan"),
        P("seq", "chan"),
        P("seq", "chan"),
        P("seq", "chan"),
        P("chan"),
        P("chan", None),
    )
    return jax.shard_map(
        on_device, mesh=mesh, in_specs=in_specs, out_specs=P("seq", "chan"), check_vma=False
    )
```

```python
import jax
import jax.numpy as jnp
import ml_dtypes
import numpy as np
from jax import lax
from jax.experimental import pallas as pl
from jax.experimental.pallas import tpu as pltpu
from jax.sharding import PartitionSpec as P

LANES = 128
F32 = jnp.float32
BF16 = jnp.bfloat16
SMALL_VMEM = 16 * 1024 * 1024
VMEM_BYTES = 24 * 1024 * 1024
GROUP = 16
SIDE = 4
CORES = 2


def halves(table):
    head = table.astype(ml_dtypes.bfloat16)
    tail = (table - head.astype(np.float64)).astype(ml_dtypes.bfloat16)
    return head, tail


def exchange_order(n_parts):
    gray = (0, 1, 3, 2)
    order = [(y * SIDE + gray[x]) * CORES + c for y in range(SIDE) for x in range(SIDE) for c in range(CORES)]
    return order if len(order) == n_parts else list(range(n_parts))


def exchange(value, n_parts):
    groups = [exchange_order(n_parts)]
    return lax.all_to_all(value, "seq", split_axis=0, concat_axis=0, tiled=True, axis_index_groups=groups)


def transform_tables(n_parts):
    size = LANES
    total = size * size
    place = np.arange(size)
    pieces = size // n_parts
    a_of = pieces * np.array(exchange_order(n_parts))[place % n_parts] + place // n_parts
    k1 = np.arange(size)
    coarse = -2.0 * np.pi * ((a_of[None, :] * (4 * k1[:, None] + 1)) % (4 * size)) / (4 * size)
    first = np.concatenate([np.cos(coarse), np.sin(coarse)], 0)
    b_of = np.arange(size)
    turn = -2.0 * np.pi * ((b_of[None, :] * (4 * k1[:, None] + 1)) % (4 * total)) / (4 * total)
    fine = -2.0 * np.pi * ((b_of[:, None] * k1[None, :]) % size) / size
    cos_f, sin_f = np.cos(fine), np.sin(fine)
    second = np.block([[cos_f, sin_f], [-sin_f, cos_f]])
    second_back = np.block([[cos_f.T, -sin_f.T], [sin_f.T, cos_f.T]])
    first_back = np.concatenate([np.cos(coarse).T, np.sin(coarse).T], 1) / total
    return first, np.cos(turn), np.sin(turn), second, second_back, first_back


def split(value):
    head = value.astype(BF16)
    return head, (value - head.astype(F32)).astype(BF16)


def dot(left, right):
    return jnp.dot(left, right, preferred_element_type=F32)


def tables_of(n_parts):
    first, turn_cos, turn_sin, second, second_back, first_back = transform_tables(n_parts)

    def left(table):
        high, low = halves(table)
        return jnp.asarray(np.concatenate([high, low, high], 1))

    def right(table):
        high, low = halves(table)
        return jnp.asarray(np.concatenate([high, low, high], 0))

    turns = [jnp.asarray(turn_cos.astype(np.float32)), jnp.asarray(turn_sin.astype(np.float32))]
    return [left(first), *turns, right(second), right(second_back), left(first_back)]


def from_left(table, value):
    high, low = split(value)
    return dot(table, jnp.concatenate([high, high, low], 0))


def from_right(value, table):
    high, low = split(value)
    return dot(jnp.concatenate([high, high, low], 1), table)


def pack_kernel(key_ref, value_ref, taps_ref, out_ref, key_vmem, value_vmem, taps_vmem, sems):
    parts, _, pieces, width, _ = out_ref.shape
    pairs = ((key_ref, key_vmem), (value_ref, value_vmem), (taps_ref, taps_vmem))
    rows = [pl.ds(j * LANES, LANES) for j in range(pieces)]
    copies = [
        [pltpu.make_async_copy(x.at[at], y.at[at], sems.at[k, j]) for k, (x, y) in enumerate(pairs)]
        for j, at in enumerate(rows)
    ]
    for piece in copies:
        for copy in piece:
            copy.start()
    for j, at in enumerate(rows):
        for copy in copies[j]:
            copy.wait()
        signal = key_vmem[at].astype(F32) * value_vmem[at].astype(F32)
        out_ref[:, 0, j] = signal.T.reshape(parts, width, LANES)
        out_ref[:, 1, j] = taps_vmem[at].T.reshape(parts, width, LANES)


def pack(key_in, value_in, filter_taps, n_parts):
    tok_rows, span = key_in.shape
    pieces = tok_rows // LANES
    arrays = (key_in, value_in, filter_taps)
    return pl.pallas_call(
        pack_kernel,
        in_specs=[pl.BlockSpec(memory_space=pltpu.HBM)] * 3,
        out_specs=pl.BlockSpec(memory_space=pltpu.VMEM),
        out_shape=jax.ShapeDtypeStruct((n_parts, 2, pieces, span // n_parts, LANES), F32),
        scratch_shapes=[pltpu.VMEM(x.shape, x.dtype) for x in arrays]
        + [pltpu.SemaphoreType.DMA((3, pieces))],
        compiler_params=pltpu.CompilerParams(vmem_limit_bytes=SMALL_VMEM),
        name="pack",
    )(*(pltpu.with_memory_space_constraint(x, pltpu.HBM) for x in arrays))


def conv_kernel(n_parts, width, group, x_ref, first_ref, cos_ref, sin_ref, second_ref, back2_ref, back1_ref, out_ref):
    pieces = LANES // n_parts
    rows = pieces * width
    cos_t, sin_t = cos_ref[...], sin_ref[...]

    def column(part, channel):
        return jnp.concatenate(
            [
                x_ref[pl.ds(part * rows + j * width + channel, n_parts, stride=2 * rows), :]
                for j in range(pieces)
            ],
            0,
        )

    def spectrum(coarse, lane):
        real = coarse[:LANES, lane : lane + LANES]
        imag = coarse[LANES:, lane : lane + LANES]
        return jnp.concatenate([real * cos_t - imag * sin_t, real * sin_t + imag * cos_t], 1)

    def product(pair):
        s_re, s_im = pair[:LANES, :LANES], pair[:LANES, LANES:]
        h_re, h_im = pair[LANES:, :LANES], pair[LANES:, LANES:]
        return jnp.concatenate([s_re * h_re - s_im * h_im, s_re * h_im + s_im * h_re], 1)

    def unturn(back):
        real, imag = back[:, :LANES], back[:, LANES:]
        return jnp.concatenate([real * cos_t + imag * sin_t, imag * cos_t - real * sin_t], 0)

    @pl.loop(0, width // group)
    def _(turn):
        channels = [turn * group + i for i in range(group)]
        coarse = [
            from_left(first_ref[...], jnp.concatenate([column(0, c), column(1, c)], 1))
            for c in channels
        ]
        turned = [jnp.concatenate([spectrum(c, lane) for lane in (0, LANES)], 0) for c in coarse]
        full = [from_right(t, second_ref[...]) for t in turned]
        back = [from_right(product(f), back2_ref[...]) for f in full]
        result = from_left(back1_ref[...], jnp.concatenate([unturn(b) for b in back], 1))
        for k, channel in enumerate(channels):
            for j in range(pieces):
                out_ref[pl.ds(j * width + channel, n_parts, stride=rows), :] = result[
                    j * n_parts : (j + 1) * n_parts, k * LANES : (k + 1) * LANES
                ]


def convolve(moved, n_parts, width):
    pieces = LANES // n_parts
    group = GROUP if width % GROUP == 0 else 1
    flops = 2 * 3 * LANES * LANES * LANES * width * 18
    return pl.pallas_call(
        lambda *refs: conv_kernel(n_parts, width, group, *refs),
        out_shape=jax.ShapeDtypeStruct((n_parts * pieces * width, LANES), F32),
        compiler_params=pltpu.CompilerParams(vmem_limit_bytes=VMEM_BYTES),
        cost_estimate=pl.CostEstimate(flops=flops, bytes_accessed=moved.size * 6, transcendentals=0),
        name="convolve",
    )(moved, *tables_of(n_parts))


def gate_kernel(conv_ref, query_ref, key_ref, value_ref, gain_ref, out_ref):
    parts, pieces, width, _ = conv_ref.shape
    for j in range(pieces):
        at = slice(j * LANES, (j + 1) * LANES)
        conv = conv_ref[:, j].reshape(parts * width, LANES).T
        signal = key_ref[at].astype(F32) * value_ref[at].astype(F32)
        response = conv + gain_ref[...] * signal
        out_ref[at] = (query_ref[at].astype(F32) * response).astype(BF16)


def gate(conv, query_in, key_in, value_in, skip_gain):
    whole = pl.BlockSpec(memory_space=pltpu.VMEM)
    return pl.pallas_call(
        gate_kernel,
        in_specs=[whole] * 5,
        out_specs=whole,
        out_shape=jax.ShapeDtypeStruct(query_in.shape, BF16),
        compiler_params=pltpu.CompilerParams(vmem_limit_bytes=SMALL_VMEM),
        name="gate",
    )(conv, query_in, key_in, value_in, skip_gain.reshape(1, query_in.shape[1]))


def columns_kernel(_, weight_ref, out_ref):
    out_ref[...] = weight_ref[...]


def columns(out_weight, device, out_cols):
    rows = out_weight.shape[0]
    return pl.pallas_call(
        columns_kernel,
        grid_spec=pltpu.PrefetchScalarGridSpec(
            num_scalar_prefetch=1,
            grid=(1,),
            in_specs=[pl.BlockSpec((rows, out_cols), lambda i, at: (0, at[0]))],
            out_specs=pl.BlockSpec((rows, out_cols), lambda i, at: (0, 0)),
        ),
        out_shape=jax.ShapeDtypeStruct((rows, out_cols), out_weight.dtype),
        compiler_params=pltpu.CompilerParams(vmem_limit_bytes=SMALL_VMEM),
        name="columns",
    )(device.astype(jnp.int32).reshape(1), pltpu.with_memory_space_constraint(out_weight, pltpu.HBM))


def ring_sum(gated, weights, way, start):
    n_chan = len(weights)
    hops = [(i, (i + way) % n_chan) for i in range(n_chan)]
    total = dot(gated, weights[way * start % n_chan])
    for ahead in range(start - 1, -1, -1):
        got = lax.ppermute(total, "chan", hops)
        if ahead == 0:
            return got
        got, gated = lax.optimization_barrier((got, gated))
        total = got + dot(gated, weights[way * ahead % n_chan])


def join_kernel(upper_ref, lower_ref, out_ref):
    half = upper_ref.shape[0]
    out_ref[:half] = upper_ref[...]
    out_ref[half:] = lower_ref[...]


def join(upper, lower):
    whole = pl.BlockSpec(memory_space=pltpu.VMEM)
    return pl.pallas_call(
        join_kernel,
        in_specs=[whole] * 2,
        out_specs=whole,
        out_shape=jax.ShapeDtypeStruct((2 * upper.shape[0], upper.shape[1]), upper.dtype),
        compiler_params=pltpu.CompilerParams(vmem_limit_bytes=SMALL_VMEM),
        name="join",
    )(upper, lower)


def on_device(query_in, key_in, value_in, filter_taps, skip_gain, out_weight):
    n_parts = lax.axis_size("seq")
    n_chan = lax.axis_size("chan")
    tok_rows, channels = key_in.shape
    pieces = tok_rows // LANES
    width = channels // n_parts
    packed = pack(key_in, value_in, filter_taps, n_parts)
    moved = exchange(packed, n_parts)
    conv = convolve(moved.reshape(-1, LANES), n_parts, width)
    conv = conv.reshape(n_parts, pieces, width, LANES)
    me = lax.axis_index("chan")
    out_cols = out_weight.shape[1] // n_chan
    weights = [
        lax.dynamic_slice(out_weight, (0, (me + k) % n_chan * out_cols), (channels, out_cols))
        for k in range(n_chan)
    ]
    weights[n_chan // 2] = columns(out_weight, (me + n_chan // 2) % n_chan, out_cols)
    conv = exchange(conv, n_parts)
    conv, weights = lax.optimization_barrier((conv, weights))
    gated = gate(conv, query_in, key_in, value_in, skip_gain)
    rows = []
    half, far = tok_rows // 2, n_chan // 2
    for block, starts in ((gated[:half], (far, far - 1)), (gated[half:], (far - 1, far))):
        up, down = [ring_sum(block, weights, way, start) for way, start in zip((1, -1), starts)]
        up, down, block = lax.optimization_barrier((up, down, block))
        rows.append((up + down + dot(block, weights[0])).astype(BF16))
    return join(*rows)


def solution(mesh):
    in_specs = (
        P("seq", "chan"),
        P("seq", "chan"),
        P("seq", "chan"),
        P("seq", "chan"),
        P("chan"),
        P("chan", None),
    )
    return jax.shard_map(
        on_device, mesh=mesh, in_specs=in_specs, out_specs=P("seq", "chan"), check_vma=False
    )
```

```python
import jax
import jax.numpy as jnp
import ml_dtypes
import numpy as np
from jax import lax
from jax.experimental import pallas as pl
from jax.experimental.pallas import tpu as pltpu
from jax.sharding import PartitionSpec as P

LANES = 128
F32 = jnp.float32
BF16 = jnp.bfloat16
SMALL_VMEM = 16 * 1024 * 1024
VMEM_BYTES = 24 * 1024 * 1024
GROUP = 16
SIDE = 4
CORES = 2


def halves(table):
    head = table.astype(ml_dtypes.bfloat16)
    tail = (table - head.astype(np.float64)).astype(ml_dtypes.bfloat16)
    return head, tail


def exchange_order(n_parts):
    gray = (0, 1, 3, 2)
    order = [(y * SIDE + gray[x]) * CORES + c for c in range(CORES) for y in range(SIDE) for x in range(SIDE)]
    return order if len(order) == n_parts else list(range(n_parts))


def exchange(value, n_parts):
    groups = [exchange_order(n_parts)]
    return lax.all_to_all(value, "seq", split_axis=0, concat_axis=0, tiled=True, axis_index_groups=groups)


def transform_tables(n_parts):
    size = LANES
    total = size * size
    place = np.arange(size)
    pieces = size // n_parts
    a_of = pieces * np.array(exchange_order(n_parts))[place % n_parts] + place // n_parts
    k1 = np.arange(size)
    coarse = -2.0 * np.pi * ((a_of[None, :] * (4 * k1[:, None] + 1)) % (4 * size)) / (4 * size)
    first = np.concatenate([np.cos(coarse), np.sin(coarse)], 0)
    b_of = np.arange(size)
    turn = -2.0 * np.pi * ((b_of[None, :] * (4 * k1[:, None] + 1)) % (4 * total)) / (4 * total)
    fine = -2.0 * np.pi * ((b_of[:, None] * k1[None, :]) % size) / size
    cos_f, sin_f = np.cos(fine), np.sin(fine)
    second = np.block([[cos_f, sin_f], [-sin_f, cos_f]])
    second_back = np.block([[cos_f.T, -sin_f.T], [sin_f.T, cos_f.T]])
    first_back = np.concatenate([np.cos(coarse).T, np.sin(coarse).T], 1) / total
    return first, np.cos(turn), np.sin(turn), second, second_back, first_back


def split(value):
    head = value.astype(BF16)
    return head, (value - head.astype(F32)).astype(BF16)


def dot(left, right):
    return jnp.dot(left, right, preferred_element_type=F32)


def tables_of(n_parts):
    first, turn_cos, turn_sin, second, second_back, first_back = transform_tables(n_parts)

    def left(table):
        high, low = halves(table)
        return jnp.asarray(np.concatenate([high, low, high], 1))

    def right(table):
        high, low = halves(table)
        return jnp.asarray(np.concatenate([high, low, high], 0))

    turns = [jnp.asarray(turn_cos.astype(np.float32)), jnp.asarray(turn_sin.astype(np.float32))]
    return [left(first), *turns, right(second), right(second_back), left(first_back)]


def from_left(table, value):
    high, low = split(value)
    return dot(table, jnp.concatenate([high, high, low], 0))


def from_right(value, table):
    high, low = split(value)
    return dot(jnp.concatenate([high, high, low], 1), table)


def pack_kernel(key_ref, value_ref, taps_ref, out_ref, key_vmem, value_vmem, taps_vmem, sems):
    parts, _, pieces, width, _ = out_ref.shape
    pairs = ((key_ref, key_vmem), (value_ref, value_vmem), (taps_ref, taps_vmem))
    rows = [pl.ds(j * LANES, LANES) for j in range(pieces)]
    copies = [
        [pltpu.make_async_copy(x.at[at], y.at[at], sems.at[k, j]) for k, (x, y) in enumerate(pairs)]
        for j, at in enumerate(rows)
    ]
    for piece in copies:
        for copy in piece:
            copy.start()
    for j, at in enumerate(rows):
        for copy in copies[j]:
            copy.wait()
        signal = key_vmem[at].astype(F32) * value_vmem[at].astype(F32)
        out_ref[:, 0, j] = signal.T.reshape(parts, width, LANES)
        out_ref[:, 1, j] = taps_vmem[at].T.reshape(parts, width, LANES)


def pack(key_in, value_in, filter_taps, n_parts):
    tok_rows, span = key_in.shape
    pieces = tok_rows // LANES
    arrays = (key_in, value_in, filter_taps)
    return pl.pallas_call(
        pack_kernel,
        in_specs=[pl.BlockSpec(memory_space=pltpu.HBM)] * 3,
        out_specs=pl.BlockSpec(memory_space=pltpu.VMEM),
        out_shape=jax.ShapeDtypeStruct((n_parts, 2, pieces, span // n_parts, LANES), F32),
        scratch_shapes=[pltpu.VMEM(x.shape, x.dtype) for x in arrays]
        + [pltpu.SemaphoreType.DMA((3, pieces))],
        compiler_params=pltpu.CompilerParams(vmem_limit_bytes=SMALL_VMEM),
        name="pack",
    )(*(pltpu.with_memory_space_constraint(x, pltpu.HBM) for x in arrays))


def conv_kernel(n_parts, width, group, x_ref, first_ref, cos_ref, sin_ref, second_ref, back2_ref, back1_ref, out_ref):
    pieces = LANES // n_parts
    rows = pieces * width
    cos_t, sin_t = cos_ref[...], sin_ref[...]

    def column(part, channel):
        return jnp.concatenate(
            [
                x_ref[pl.ds(part * rows + j * width + channel, n_parts, stride=2 * rows), :]
                for j in range(pieces)
            ],
            0,
        )

    def spectrum(coarse, lane):
        real = coarse[:LANES, lane : lane + LANES]
        imag = coarse[LANES:, lane : lane + LANES]
        return jnp.concatenate([real * cos_t - imag * sin_t, real * sin_t + imag * cos_t], 1)

    def product(pair):
        s_re, s_im = pair[:LANES, :LANES], pair[:LANES, LANES:]
        h_re, h_im = pair[LANES:, :LANES], pair[LANES:, LANES:]
        return jnp.concatenate([s_re * h_re - s_im * h_im, s_re * h_im + s_im * h_re], 1)

    def unturn(back):
        real, imag = back[:, :LANES], back[:, LANES:]
        return jnp.concatenate([real * cos_t + imag * sin_t, imag * cos_t - real * sin_t], 0)

    @pl.loop(0, width // group)
    def _(turn):
        channels = [turn * group + i for i in range(group)]
        coarse = [
            from_left(first_ref[...], jnp.concatenate([column(0, c), column(1, c)], 1))
            for c in channels
        ]
        turned = [jnp.concatenate([spectrum(c, lane) for lane in (0, LANES)], 0) for c in coarse]
        full = [from_right(t, second_ref[...]) for t in turned]
        back = [from_right(product(f), back2_ref[...]) for f in full]
        result = from_left(back1_ref[...], jnp.concatenate([unturn(b) for b in back], 1))
        for k, channel in enumerate(channels):
            for j in range(pieces):
                out_ref[pl.ds(j * width + channel, n_parts, stride=rows), :] = result[
                    j * n_parts : (j + 1) * n_parts, k * LANES : (k + 1) * LANES
                ]


def convolve(moved, n_parts, width):
    pieces = LANES // n_parts
    group = GROUP if width % GROUP == 0 else 1
    flops = 2 * 3 * LANES * LANES * LANES * width * 18
    return pl.pallas_call(
        lambda *refs: conv_kernel(n_parts, width, group, *refs),
        out_shape=jax.ShapeDtypeStruct((n_parts * pieces * width, LANES), F32),
        compiler_params=pltpu.CompilerParams(vmem_limit_bytes=VMEM_BYTES),
        cost_estimate=pl.CostEstimate(flops=flops, bytes_accessed=moved.size * 6, transcendentals=0),
        name="convolve",
    )(moved, *tables_of(n_parts))


def gate_kernel(conv_ref, query_ref, key_ref, value_ref, gain_ref, out_ref):
    parts, pieces, width, _ = conv_ref.shape
    for j in range(pieces):
        at = slice(j * LANES, (j + 1) * LANES)
        conv = conv_ref[:, j].reshape(parts * width, LANES).T
        signal = key_ref[at].astype(F32) * value_ref[at].astype(F32)
        response = conv + gain_ref[...] * signal
        out_ref[at] = (query_ref[at].astype(F32) * response).astype(BF16)


def gate(conv, query_in, key_in, value_in, skip_gain):
    whole = pl.BlockSpec(memory_space=pltpu.VMEM)
    return pl.pallas_call(
        gate_kernel,
        in_specs=[whole] * 5,
        out_specs=whole,
        out_shape=jax.ShapeDtypeStruct(query_in.shape, BF16),
        compiler_params=pltpu.CompilerParams(vmem_limit_bytes=SMALL_VMEM),
        name="gate",
    )(conv, query_in, key_in, value_in, skip_gain.reshape(1, query_in.shape[1]))


def columns_kernel(_, weight_ref, out_ref):
    out_ref[...] = weight_ref[...]


def columns(out_weight, device, out_cols):
    rows = out_weight.shape[0]
    return pl.pallas_call(
        columns_kernel,
        grid_spec=pltpu.PrefetchScalarGridSpec(
            num_scalar_prefetch=1,
            grid=(1,),
            in_specs=[pl.BlockSpec((rows, out_cols), lambda i, at: (0, at[0]))],
            out_specs=pl.BlockSpec((rows, out_cols), lambda i, at: (0, 0)),
        ),
        out_shape=jax.ShapeDtypeStruct((rows, out_cols), out_weight.dtype),
        compiler_params=pltpu.CompilerParams(vmem_limit_bytes=SMALL_VMEM),
        name="columns",
    )(device.astype(jnp.int32).reshape(1), pltpu.with_memory_space_constraint(out_weight, pltpu.HBM))


def ring_sum(gated, weights, way, start):
    n_chan = len(weights)
    hops = [(i, (i + way) % n_chan) for i in range(n_chan)]
    total = dot(gated, weights[way * start % n_chan])
    for ahead in range(start - 1, -1, -1):
        got = lax.ppermute(total, "chan", hops)
        if ahead == 0:
            return got
        got, gated = lax.optimization_barrier((got, gated))
        total = got + dot(gated, weights[way * ahead % n_chan])


def join_kernel(upper_ref, lower_ref, out_ref):
    half = upper_ref.shape[0]
    out_ref[:half] = upper_ref[...]
    out_ref[half:] = lower_ref[...]


def join(upper, lower):
    whole = pl.BlockSpec(memory_space=pltpu.VMEM)
    return pl.pallas_call(
        join_kernel,
        in_specs=[whole] * 2,
        out_specs=whole,
        out_shape=jax.ShapeDtypeStruct((2 * upper.shape[0], upper.shape[1]), upper.dtype),
        compiler_params=pltpu.CompilerParams(vmem_limit_bytes=SMALL_VMEM),
        name="join",
    )(upper, lower)


def on_device(query_in, key_in, value_in, filter_taps, skip_gain, out_weight):
    n_parts = lax.axis_size("seq")
    n_chan = lax.axis_size("chan")
    tok_rows, channels = key_in.shape
    pieces = tok_rows // LANES
    width = channels // n_parts
    packed = pack(key_in, value_in, filter_taps, n_parts)
    moved = exchange(packed, n_parts)
    conv = convolve(moved.reshape(-1, LANES), n_parts, width)
    conv = conv.reshape(n_parts, pieces, width, LANES)
    me = lax.axis_index("chan")
    out_cols = out_weight.shape[1] // n_chan
    weights = [
        lax.dynamic_slice(out_weight, (0, (me + k) % n_chan * out_cols), (channels, out_cols))
        for k in range(n_chan)
    ]
    weights[n_chan // 2] = columns(out_weight, (me + n_chan // 2) % n_chan, out_cols)
    conv = exchange(conv, n_parts)
    conv, weights = lax.optimization_barrier((conv, weights))
    gated = gate(conv, query_in, key_in, value_in, skip_gain)
    rows = []
    half, far = tok_rows // 2, n_chan // 2
    for block, starts in ((gated[:half], (far, far - 1)), (gated[half:], (far - 1, far))):
        up, down = [ring_sum(block, weights, way, start) for way, start in zip((1, -1), starts)]
        up, down, block = lax.optimization_barrier((up, down, block))
        rows.append((up + down + dot(block, weights[0])).astype(BF16))
    return join(*rows)


def solution(mesh):
    in_specs = (
        P("seq", "chan"),
        P("seq", "chan"),
        P("seq", "chan"),
        P("seq", "chan"),
        P("chan"),
        P("chan", None),
    )
    return jax.shard_map(
        on_device, mesh=mesh, in_specs=in_specs, out_specs=P("seq", "chan"), check_vma=False
    )
```
